256 devices in a mesh: blk: 32 (over z, y_hi, core), dp: 8 (over x, y_lo).
Axes of the slice: x: 4, y: 4 (y_hi: 2, y_lo: 2; y = y_hi * 2 + y_lo), z: 8, core: 2. Of those that a mesh axis runs over, the one named last changes fastest.
Arguments:
- tokens: bfloat16 [65536, 4096], P(('blk', 'dp')), may hold values from -6 to 6
- cotangent: bfloat16 [65536, 4096], P(('blk', 'dp')), may hold values from -6 to 6
- gain: float32 [4096], replicated, may hold values from 0.1 to 1.9
- gate_up: bfloat16 [4096, 12288], P(None, 'blk'), may hold values from -0.09375 to 0.09375
- down: bfloat16 [6144, 4096], P('blk'), may hold values from -0.078125 to 0.078125
Outputs:
- grad_gate_up: float32 [4096, 12288], P('dp', 'blk')
- grad_down: float32 [6144, 4096], P('blk', 'dp')
The draws below stay inside these ranges and needn't reach their ends.
All inputs are finite; a program needn't handle non-finite values.
Results may differ from the reference program's by a relative error of at most 0.0059.
Values may be sent and summed in bfloat16 or wider, within the bound.
A program may use at most 64 MiB of HBM per device.

```python
import math
import jax
import jax.numpy as jnp
from jax import lax

D = 4096
FB = 192
TOK_DEV = 256
FF = 6144
ROWS = 65536
N_BLK = 32
N_DP = 8


def block_levels(rng, extent, split, smallest, largest):
    def one(position, shards_of):
        heights = jax.random.uniform(jax.random.fold_in(jax.random.fold_in(rng, 6), position), (shards_of,), jnp.float32, smallest / len(split), largest / len(split))
        return jnp.repeat(jnp.exp(heights), extent[position] // shards_of).reshape((-1,) + (1,) * (len(extent) - position - 1))

    loudness = one(*split[0])
    for cut in split[1:]:
        loudness = loudness * one(*cut)
    return loudness


def noise(key, extent, deviation, reach, shards=(), kind=jnp.bfloat16):
    array = jax.random.normal(key, extent, jnp.float32) * deviation
    if len(shards) > 0:
        array = block_levels(key, extent, shards, -0.22, 0.18) * array
    return jnp.clip(array, min=-reach, max=reach).astype(kind)


def setup_inputs(seed: int = 0) -> dict:
    arg_keys = jax.random.split(jax.random.key(seed), 6)
    return {
        "tokens": noise(arg_keys[0], (ROWS, D), 1.0, 6.0, ((0, 256),)),
        "cotangent": noise(arg_keys[1], (ROWS, D), 1.0, 6.0, ((0, 256),)),
        "gain": jnp.clip(1.0 + 0.18 * jax.random.normal(arg_keys[2], (D,), jnp.float32), 0.1, 1.9),
        "gate_up": noise(arg_keys[3], (D, 2 * FF), D ** -0.5, 0.09375, ((1, 32),)),
        "down": noise(arg_keys[4], (FF, D), (FB * N_BLK) ** -0.5, 0.078125, ((0, 32),)),
    }


def shard_grads(rows, upstream, gain, gate_up, down, factor):
    values = rows.astype(jnp.float32)
    inverse = lax.rsqrt(lax.optimization_barrier(jnp.mean(values * values, axis=-1, keepdims=True)) + 1e-06)
    normal_rows = (values * inverse * gain).astype(jnp.bfloat16)
    width = down.shape[0]
    projected = jnp.einsum('ptd,df->ptf', normal_rows.astype(jnp.float32), gate_up.astype(jnp.float32))
    gate = projected[..., :width]
    upward = projected[..., width:]
    sigmoid_gate = jax.nn.sigmoid(gate)
    hidden = (gate * sigmoid_gate * upward).astype(jnp.bfloat16)
    back = jnp.einsum('ptd,fd->ptf', upstream.astype(jnp.float32), down.astype(jnp.float32))
    slope = sigmoid_gate * (1.0 + gate * (1.0 - sigmoid_gate))
    back_gate_up = jnp.concatenate([back * upward * slope, back * gate * sigmoid_gate], axis=-1).astype(jnp.bfloat16)
    grad_gate_up = jnp.einsum('ptd,ptf->pdf', normal_rows.astype(jnp.float32), back_gate_up.astype(jnp.float32)) * factor
    grad_down = jnp.einsum('ptf,ptd->pfd', hidden.astype(jnp.float32), upstream.astype(jnp.float32)) * factor
    return (grad_gate_up, grad_down)

def rounded(values):
    return lax.optimization_barrier(values.astype(jnp.bfloat16)).astype(jnp.float32)

def reference(tokens, cotangent, gain, gate_up, down):
    factor = 1.0 / math.sqrt(3 * TOK_DEV * N_DP)
    blocks = tokens.reshape(N_BLK, N_DP, TOK_DEV, D)
    upstream = cotangent.reshape(N_BLK, N_DP, TOK_DEV, D)
    shards_gu = gate_up.reshape(D, N_BLK, 2 * FB).transpose(1, 0, 2)
    shards_down = down.reshape(N_BLK, FB, D)

    def per_shard(shard):
        weights_gu = shards_gu[shard]
        weights_down = shards_down[shard]

        def contrib(offset):
            index = ((shard + offset) % N_BLK).astype(jnp.int32)
            return shard_grads(blocks[index], upstream[index], gain, weights_gu, weights_down, factor)
        running = contrib(2)
        for offset in (1, 0):
            terms = contrib(offset)
            running = (rounded(running[0]) + terms[0], rounded(running[1]) + terms[1])
        return (lax.optimization_barrier(jnp.sum(running[0], axis=0)), lax.optimization_barrier(jnp.sum(running[1], axis=0)))
    grads_gu, grads_down = lax.map(per_shard, jnp.arange(N_BLK, dtype=jnp.int32))
    grad_gate_up = grads_gu.transpose(1, 0, 2).reshape(D, 2 * FF)
    grad_down = grads_down.reshape(FF, D)
    return (grad_gate_up, grad_down)
```

```python
import functools
import math

import jax
import jax.numpy as jnp
from jax import lax
from jax.experimental import pallas as pl
from jax.experimental.pallas import tpu as pltpu
from jax.sharding import PartitionSpec as P

MESH = pl.DeviceIdType.MESH
F32 = jnp.float32
BF16 = jnp.bfloat16

TOK = 256
D = 4096
FB = 192
SL = D // 8
CH = 64
NCH = TOK // CH

ORDERS = (("a", "b", "y"), ("b", "y", "a"), ("y", "a", "b"))


def flip(v):
    return v + 1 - 2 * lax.rem(v, 2)


def moved(d, toggle):
    x, y = d // 2, lax.rem(d, 2)
    x = x + toggle["a"] * (1 - 2 * lax.rem(x, 2))
    x = lax.rem(x + toggle["b"] * (2 * lax.rem(x, 2) - 1) + 4, 4)
    y = y + toggle["y"] * (1 - 2 * y)
    return 2 * x + y


def partner(d, dim):
    return moved(d, {name: int(name == dim) for name in "aby"})


def share_rs(d, p, r):
    o = ORDERS[p]
    return moved(d, {o[0]: r // 4, o[1]: lax.rem(r // 2, 2), o[2]: lax.rem(r, 2)})


def share_ag(d, p, r):
    o = ORDERS[p]
    return moved(d, {o[2]: r // 4, o[1]: lax.rem(r // 2, 2), o[0]: lax.rem(r, 2)})


def columns(j, width):
    return pl.ds(pl.multiple_of(j * width, width), width)


def kernel(
    scale,
    tok, cot, gain, gu, dn,
    o_gu, o_dn,
    nrm, ctg, wg, wd, wf, wfd, proj, act, actf, snd, rcv, rcvf, acc, back, ret,
    ld_sem, ws_s, ws_r, ag_s, ag_r, rs_s, rs_r, rf_s, rf_r,
    tk_s, tk_r, fw_s, fw_r, t1_s, t1_r, rt_s, rt_r,
):
    b = lax.axis_index("blk")
    d = lax.axis_index("dp")
    core = lax.rem(b, 2)
    n_blk = 32
    nxt = lax.rem(b + 2, n_blk)
    prv = lax.rem(b + n_blk - 2, n_blk)
    other = flip(b)
    df = flip(d)
    own = pl.ds(pl.multiple_of(core * TOK, TOK), TOK)

    def load(i, src, dst):
        return pltpu.make_async_copy(src, dst, ld_sem.at[i])

    def remote(src, dst, ss, rs, tb, td):
        return pltpu.make_async_remote_copy(
            src_ref=src, dst_ref=dst, send_sem=ss, recv_sem=rs,
            device_id=(tb, td), device_id_type=MESH,
        )

    ld_tok = load(0, tok, nrm.at[own])
    ld_cot = load(1, cot, ctg.at[own])
    ld_wg = load(2, gu, wg)
    ld_wd = load(3, dn, wd)
    ld_tok.start()
    ld_cot.start()
    ld_wg.start()
    ld_wd.start()

    barrier = pltpu.get_barrier_semaphore()
    greeted = [(other, d), (nxt, df), (prv, df)] + [(b, partner(d, k)) for k in "aby"]
    for tb, td in greeted:
        pl.semaphore_signal(barrier, inc=1, device_id=(tb, td), device_id_type=MESH)
    pl.semaphore_wait(barrier, len(greeted))

    def weight_slice(p):
        if p == 2:
            return remote(dn.at[:, columns(df, SL)], wfd.at[0], ws_s.at[2], ws_r.at[2], nxt, df)
        rows = pl.ds(pl.multiple_of(df * SL + p * 256, 256), 256)
        return remote(gu.at[rows, :], wf.at[p, 0], ws_s.at[p], ws_r.at[p], nxt, df)

    def gather(p, step):
        n = 2 ** step
        ref = wfd if p == 2 else wf.at[p]
        return remote(
            ref.at[pl.ds(0, n)], ref.at[pl.ds(n, n)],
            ag_s.at[p, step], ag_r.at[p, step], b, partner(d, ORDERS[p][step]),
        )

    def token_piece(i, kind):
        here = pl.ds(pl.multiple_of(i * CH, CH), CH)
        there = pl.ds(pl.multiple_of(2 * TOK + i * CH, CH), CH)
        if kind == 0:
            return remote(cot.at[here], ctg.at[there], tk_s.at[i, 0], tk_r.at[i, 0], prv, df)
        return remote(nrm.at[here], nrm.at[there], tk_s.at[i, 1], tk_r.at[i, 1], prv, df)

    def forwarded(i, kind):
        there = pl.ds(pl.multiple_of(2 * TOK + i * CH, CH), CH)
        ref = nrm if kind else ctg
        return remote(ref.at[there], ref.at[there], fw_s.at[i, kind], fw_r.at[i, kind], other, d)

    mid = pl.ds(TOK, TOK)
    mid_cot = remote(cot, ctg.at[mid], t1_s.at[0], t1_r.at[0], other, d)
    mid_nrm = remote(nrm.at[mid], nrm.at[mid], t1_s.at[1], t1_r.at[1], other, d)

    def returned(p):
        return remote(back.at[p], ret.at[p], rt_s.at[p], rt_r.at[p], prv, df)

    def normalise(row0, n):
        def body(i, _):
            rows = pl.ds(pl.multiple_of(row0 + i * 16, 16), 16)
            v = nrm[rows, :].astype(F32)
            inv = lax.rsqrt(jnp.mean(v * v, axis=-1, keepdims=True) + 1e-06)
            nrm[rows, :] = (v * inv * gain[...]).astype(BF16)
            return 0

        lax.fori_loop(0, n // 16, body, 0)

    def forward(row0, n, to):
        rows = pl.ds(pl.multiple_of(row0, CH), n)
        out = pl.ds(pl.multiple_of(to, CH), n)
        proj[out, 0:384] = jnp.dot(nrm[rows, :], wg[...], preferred_element_type=F32)
        proj[out, 384:576] = lax.dot_general(
            ctg[rows, :], wd[...], (((1,), (1,)), ((), ())), preferred_element_type=F32
        )

    def activate(dst, cols):
        t = proj[...].T
        gate, up, bk = t[0:FB], t[FB:2 * FB], t[2 * FB:3 * FB]
        s = jax.nn.sigmoid(gate)
        dst[0:FB, cols] = (bk * up * (s * (1.0 + gate * (1.0 - s)))).astype(BF16)
        dst[FB:2 * FB, cols] = (bk * gate * s).astype(BF16)
        dst[2 * FB:3 * FB, cols] = (gate * s * up).astype(BF16)

    def reduce_scatter(term, r_ref, s_sem, r_sem):
        def copy(p, slot, step):
            return remote(
                snd.at[p, slot], r_ref.at[p, slot], s_sem.at[p, slot], r_sem.at[p, slot],
                b, partner(d, ORDERS[p][step]),
            )

        def first(i, _):
            q = 3 - 2 * lax.rem(i, 2) - i // 2

            def put(p, v):
                snd[p, q] = v.astype(BF16)

            term(q + 4, put)
            for p in range(3):
                copy(p, q, 0).start()
            return 0

        def kept(i, _):
            q = 3 - 2 * lax.rem(i, 2) - i // 2

            def put(p, v):
                acc[p, q] = v

            term(q, put)
            return 0

        lax.fori_loop(0, 4, first, 0)
        lax.fori_loop(0, 4, kept, 0)
        for q in (3, 1, 2, 0):
            for p in range(3):
                copy(p, q, 0).wait_recv()
                v = acc[p, q] + r_ref[p, q].astype(F32)
                if q >= 2:
                    snd[p, q + 2] = v.astype(BF16)
                    copy(p, q + 2, 1).start()
                else:
                    acc[p, q] = v
        for p in range(3):
            copy(p, 5, 1).wait_recv()
            snd[p, 6] = (acc[p, 1] + r_ref[p, 5].astype(F32)).astype(BF16)
            copy(p, 6, 2).start()
        for p in range(3):
            copy(p, 4, 1).wait_recv()
            acc[p, 0] = acc[p, 0] + r_ref[p, 4].astype(F32)
        for p in range(3):
            copy(p, 6, 2).wait_recv()
            acc[p, 0] = acc[p, 0] + r_ref[p, 6].astype(F32)
        for p in range(3):
            for slot, step in [(k, 0) for k in range(4)] + [(4, 1), (5, 1), (6, 2)]:
                copy(p, slot, step).wait_send()

    def grads(a_ref, a_cols, tok_rows, share, put):
        for p in range(3):
            x = ctg if p == 2 else nrm
            put(p, jnp.dot(
                a_ref[p * FB:(p + 1) * FB, a_cols],
                x[tok_rows, columns(share(p), SL)],
                preferred_element_type=F32,
            ))

    @pl.when(core == 0)
    def _():
        ld_tok.wait()
        for i in range(2):
            token_piece(i, 0).start()
            normalise(i * CH, CH)
            token_piece(i, 1).start()
        normalise(2 * CH, TOK - 2 * CH)
        ld_cot.wait()
        ld_wg.wait()
        ld_wd.wait()
        forward(0, TOK, 0)
        activate(act, pl.ds(0, TOK))
        mid_cot.wait_recv()
        mid_nrm.wait_recv()
        forward(TOK, TOK, 0)
        activate(act, pl.ds(TOK, TOK))

        def piece(i, _):
            for kind in (0, 1):
                token_piece(i, kind).wait_recv()
                forwarded(i, kind).start()

            @pl.when(i + 2 < NCH)
            def _():
                for kind in (0, 1):
                    token_piece(i + 2, kind).start()

            forward(2 * TOK + i * CH, CH, i * CH)
            return 0

        lax.fori_loop(0, NCH, piece, 0)
        activate(act, pl.ds(2 * TOK, TOK))

    @pl.when(core == 1)
    def _():
        for p in range(3):
            weight_slice(p).start()
        mid_cot.start()
        ld_tok.wait()
        normalise(TOK, TOK)
        mid_nrm.start()
        for p in range(3):
            weight_slice(p).wait_recv()
            gather(p, 0).start()
        for p in range(3):
            gather(p, 0).wait_recv()
            gather(p, 1).start()
        ld_cot.wait()
        ld_wg.wait()
        ld_wd.wait()
        for p in range(3):
            gather(p, 1).wait_recv()
            gather(p, 2).start()
        forward(TOK, TOK, 0)
        activate(act, pl.ds(TOK, TOK))

        proj[...] = jnp.zeros_like(proj)

        def partial(r, _):
            for p in range(2):
                j = share_ag(d, p, r)
                cols = pl.ds(pl.multiple_of(j * SL + p * 256, 256), 256)
                proj[:, 0:384] += jnp.dot(nrm[mid, cols], wf[p, r], preferred_element_type=F32)
            proj[:, 384:576] += lax.dot_general(
                ctg[mid, columns(share_ag(d, 2, r), SL)], wfd[r],
                (((1,), (1,)), ((), ())), preferred_element_type=F32,
            )
            return 0

        lax.fori_loop(0, 4, partial, 0)
        for p in range(3):
            gather(p, 2).wait_recv()
        lax.fori_loop(4, 8, partial, 0)
        activate(actf, pl.ds(0, TOK))

        def term(r, put):
            grads(actf, slice(0, TOK), mid, lambda p: flip(share_rs(d, p, r)), put)

        reduce_scatter(term, rcvf, rf_s, rf_r)
        for p in range(3):
            back[p] = acc[p, 0].astype(BF16)
            returned(p).start()

        def piece(i, _):
            for kind in (0, 1):
                forwarded(i, kind).wait_recv()
            forward(2 * TOK + i * CH, CH, i * CH)
            return 0

        lax.fori_loop(0, NCH, piece, 0)
        activate(act, pl.ds(2 * TOK, TOK))

    def own_term(r, put):
        @pl.when(core == 0)
        def _():
            grads(act, slice(0, 3 * TOK), pl.ds(0, 3 * TOK), lambda p: share_rs(d, p, r), put)

        @pl.when(core == 1)
        def _():
            grads(act, slice(TOK, 3 * TOK), pl.ds(TOK, 2 * TOK), lambda p: share_rs(d, p, r), put)

    reduce_scatter(own_term, rcv, rs_s, rs_r)

    @pl.when(core == 1)
    def _():
        for p in range(3):
            returned(p).wait_recv()
            acc[p, 0] = acc[p, 0] + ret[p].astype(F32)

    o_gu[:, 0:FB] = (acc[0, 0] * scale).T
    o_gu[:, FB:2 * FB] = (acc[1, 0] * scale).T
    o_dn[...] = acc[2, 0] * scale

    @pl.when(core == 0)
    def _():
        for i in range(NCH):
            for kind in (0, 1):
                token_piece(i, kind).wait_send()
                forwarded(i, kind).wait_send()

    @pl.when(core == 1)
    def _():
        mid_cot.wait_send()
        mid_nrm.wait_send()
        for p in range(3):
            weight_slice(p).wait_send()
            returned(p).wait_send()
            for step in range(3):
                gather(p, step).wait_send()


def local(tokens, cotangent, gain, gate_up, down):
    scale = 1.0 / math.sqrt(3 * TOK * 8)
    anywhere = pl.BlockSpec(memory_space=pl.ANY)
    vmem = pl.BlockSpec(memory_space=pltpu.VMEM)
    dma = pltpu.SemaphoreType.DMA
    return pl.pallas_call(
        functools.partial(kernel, scale),
        out_shape=(
            jax.ShapeDtypeStruct((SL, 2 * FB), F32),
            jax.ShapeDtypeStruct((FB, SL), F32),
        ),
        in_specs=[anywhere, anywhere, vmem, anywhere, anywhere],
        out_specs=(vmem, vmem),
        scratch_shapes=[
            pltpu.VMEM((3 * TOK, D), BF16),
            pltpu.VMEM((3 * TOK, D), BF16),
            pltpu.VMEM((D, 2 * FB), BF16),
            pltpu.VMEM((FB, D), BF16),
            pltpu.VMEM((2, 8, 256, 2 * FB), BF16),
            pltpu.VMEM((8, FB, SL), BF16),
            pltpu.VMEM((TOK, 3 * FB), F32),
            pltpu.VMEM((3 * FB, 3 * TOK), BF16),
            pltpu.VMEM((3 * FB, TOK), BF16),
            pltpu.VMEM((3, 7, FB, SL), BF16),
            pltpu.VMEM((3, 7, FB, SL), BF16),
            pltpu.VMEM((3, 7, FB, SL), BF16),
            pltpu.VMEM((3, 4, FB, SL), F32),
            pltpu.VMEM((3, FB, SL), BF16),
            pltpu.VMEM((3, FB, SL), BF16),
            dma((4,)),
            dma((3,)), dma((3,)), dma((3, 3)), dma((3, 3)),
            dma((3, 7)), dma((3, 7)), dma((3, 7)), dma((3, 7)),
            dma((NCH, 2)), dma((NCH, 2)), dma((NCH, 2)), dma((NCH, 2)),
            dma((2,)), dma((2,)), dma((3,)), dma((3,)),
        ],
        compiler_params=pltpu.CompilerParams(
            collective_id=0, has_side_effects=True, vmem_limit_bytes=58 << 20
        ),
        name="grads",
    )(tokens, cotangent, gain.reshape(1, D), gate_up, down)


def solution(mesh):
    in_specs = (P(("blk", "dp"), None), P(("blk", "dp"), None), P(), P(None, "blk"), P("blk", None))
    out_specs = (P("dp", "blk"), P("blk", "dp"))
    return jax.shard_map(local, mesh=mesh, in_specs=in_specs, out_specs=out_specs, check_vma=False)
```

```python
import functools
import math

import jax
import jax.numpy as jnp
from jax import lax
from jax.experimental import pallas as pl
from jax.experimental.pallas import tpu as pltpu
from jax.sharding import PartitionSpec as P

MESH = pl.DeviceIdType.MESH
F32 = jnp.float32
BF16 = jnp.bfloat16

TOK = 256
D = 4096
FB = 192
SL = D // 8
CH = 64
NCH = TOK // CH

ORDERS = (("a", "b", "y"), ("b", "y", "a"), ("y", "a", "b"))


def flip(v):
    return v + 1 - 2 * lax.rem(v, 2)


def moved(d, toggle):
    x, y = d // 2, lax.rem(d, 2)
    x = x + toggle["a"] * (1 - 2 * lax.rem(x, 2))
    x = lax.rem(x + toggle["b"] * (2 * lax.rem(x, 2) - 1) + 4, 4)
    y = y + toggle["y"] * (1 - 2 * y)
    return 2 * x + y


def partner(d, dim):
    return moved(d, {name: int(name == dim) for name in "aby"})


def share_rs(d, p, r):
    o = ORDERS[p]
    return moved(d, {o[0]: r // 4, o[1]: lax.rem(r // 2, 2), o[2]: lax.rem(r, 2)})


def share_ag(d, p, r):
    o = ORDERS[p]
    return moved(d, {o[2]: r // 4, o[1]: lax.rem(r // 2, 2), o[0]: lax.rem(r, 2)})


def columns(j, width):
    return pl.ds(pl.multiple_of(j * width, width), width)


def kernel(
    scale,
    tok, cot, gain, gu, dn,
    o_gu, o_dn,
    nrm, ctg, wg, wd, wf, wfd, proj, act, actf, snd, rcv, rcvf, acc, back, ret,
    ld_sem, ws_s, ws_r, ag_s, ag_r, rs_s, rs_r, rf_s, rf_r,
    tk_s, tk_r, fw_s, fw_r, t1_s, t1_r, rt_s, rt_r, go,
):
    b = lax.axis_index("blk")
    d = lax.axis_index("dp")
    core = lax.rem(b, 2)
    n_blk = 32
    nxt = lax.rem(b + 2, n_blk)
    prv = lax.rem(b + n_blk - 2, n_blk)
    other = flip(b)
    beside = lax.rem(b + n_blk - 1 + 2 * core, n_blk)
    df = flip(d)
    own = pl.ds(pl.multiple_of(core * TOK, TOK), TOK)

    def load(i, src, dst):
        return pltpu.make_async_copy(src, dst, ld_sem.at[i])

    def remote(src, dst, ss, rs, tb, td):
        return pltpu.make_async_remote_copy(
            src_ref=src, dst_ref=dst, send_sem=ss, recv_sem=rs,
            device_id=(tb, td), device_id_type=MESH,
        )

    ld_tok = load(0, tok, nrm.at[own])
    ld_cot = load(1, cot, ctg.at[own])
    ld_wg = load(2, gu, wg)
    ld_wd = load(3, dn, wd)
    ld_tok.start()
    ld_cot.start()
    ld_wg.start()
    ld_wd.start()

    barrier = pltpu.get_barrier_semaphore()
    greeted = [(other, d), (nxt, df), (prv, df), (beside, df)] + [(b, partner(d, k)) for k in "aby"]
    for tb, td in greeted:
        pl.semaphore_signal(barrier, inc=1, device_id=(tb, td), device_id_type=MESH)
    pl.semaphore_wait(barrier, len(greeted))

    def weight_slice(p):
        if p == 2:
            return remote(dn.at[:, columns(df, SL)], wfd.at[0], ws_s.at[2], ws_r.at[2], nxt, df)
        rows = pl.ds(pl.multiple_of(df * SL + p * 256, 256), 256)
        return remote(gu.at[rows, :], wf.at[p, 0], ws_s.at[p], ws_r.at[p], nxt, df)

    def gather(p, step):
        n = 2 ** step
        ref = wfd if p == 2 else wf.at[p]
        return remote(
            ref.at[pl.ds(0, n)], ref.at[pl.ds(n, n)],
            ag_s.at[p, step], ag_r.at[p, step], b, partner(d, ORDERS[p][step]),
        )

    def token_piece(i, kind):
        here = pl.ds(pl.multiple_of(i * CH, CH), CH)
        there = pl.ds(pl.multiple_of(2 * TOK + i * CH, CH), CH)
        if kind == 0:
            return remote(cot.at[here], ctg.at[there], tk_s.at[i, 0], tk_r.at[i, 0], prv, df)
        return remote(nrm.at[here], nrm.at[there], tk_s.at[i, 1], tk_r.at[i, 1], prv, df)

    def forwarded(i, kind):
        there = pl.ds(pl.multiple_of(2 * TOK + i * CH, CH), CH)
        ref = nrm if kind else ctg
        return remote(ref.at[there], ref.at[there], fw_s.at[i, kind], fw_r.at[i, kind], other, d)

    mid = pl.ds(TOK, TOK)
    mid_cot = remote(cot, ctg.at[mid], t1_s.at[0], t1_r.at[0], other, d)
    mid_nrm = remote(nrm.at[mid], nrm.at[mid], t1_s.at[1], t1_r.at[1], other, d)

    def returned(p):
        return remote(back.at[p], ret.at[p], rt_s.at[p], rt_r.at[p], prv, df)

    def normalise(row0, n):
        def body(i, _):
            rows = pl.ds(pl.multiple_of(row0 + i * 16, 16), 16)
            v = nrm[rows, :].astype(F32)
            inv = lax.rsqrt(jnp.mean(v * v, axis=-1, keepdims=True) + 1e-06)
            nrm[rows, :] = (v * inv * gain[...]).astype(BF16)
            return 0

        lax.fori_loop(0, n // 16, body, 0)

    def forward(row0, n, to):
        rows = pl.ds(pl.multiple_of(row0, CH), n)
        out = pl.ds(pl.multiple_of(to, CH), n)
        proj[out, 0:384] = jnp.dot(nrm[rows, :], wg[...], preferred_element_type=F32)
        proj[out, 384:576] = lax.dot_general(
            ctg[rows, :], wd[...], (((1,), (1,)), ((), ())), preferred_element_type=F32
        )

    def activate(dst, cols):
        t = proj[...].T
        gate, up, bk = t[0:FB], t[FB:2 * FB], t[2 * FB:3 * FB]
        s = jax.nn.sigmoid(gate)
        dst[0:FB, cols] = (bk * up * (s * (1.0 + gate * (1.0 - s)))).astype(BF16)
        dst[FB:2 * FB, cols] = (bk * gate * s).astype(BF16)
        dst[2 * FB:3 * FB, cols] = (gate * s * up).astype(BF16)

    def reduce_scatter(term, r_ref, s_sem, r_sem):
        def copy(p, slot, step):
            return remote(
                snd.at[p, slot], r_ref.at[p, slot], s_sem.at[p, slot], r_sem.at[p, slot],
                b, partner(d, ORDERS[p][step]),
            )

        def first(i, _):
            q = 3 - 2 * lax.rem(i, 2) - i // 2

            def put(p, v):
                snd[p, q] = v.astype(BF16)

            term(q + 4, put)
            for p in range(3):
                copy(p, q, 0).start()
            return 0

        def kept(i, _):
            q = 3 - 2 * lax.rem(i, 2) - i // 2

            def put(p, v):
                acc[p, q] = v

            term(q, put)
            return 0

        lax.fori_loop(0, 4, first, 0)
        lax.fori_loop(0, 4, kept, 0)
        for q in (3, 1, 2, 0):
            for p in range(3):
                copy(p, q, 0).wait_recv()
                v = acc[p, q] + r_ref[p, q].astype(F32)
                if q >= 2:
                    snd[p, q + 2] = v.astype(BF16)
                    copy(p, q + 2, 1).start()
                else:
                    acc[p, q] = v
        for p in range(3):
            copy(p, 5, 1).wait_recv()
            snd[p, 6] = (acc[p, 1] + r_ref[p, 5].astype(F32)).astype(BF16)
            copy(p, 6, 2).start()
        for p in range(3):
            copy(p, 4, 1).wait_recv()
            acc[p, 0] = acc[p, 0] + r_ref[p, 4].astype(F32)
        for p in range(3):
            copy(p, 6, 2).wait_recv()
            acc[p, 0] = acc[p, 0] + r_ref[p, 6].astype(F32)
        for p in range(3):
            for slot, step in [(k, 0) for k in range(4)] + [(4, 1), (5, 1), (6, 2)]:
                copy(p, slot, step).wait_send()

    def grads(a_ref, a_cols, tok_rows, share, put):
        for p in range(3):
            x = ctg if p == 2 else nrm
            put(p, jnp.dot(
                a_ref[p * FB:(p + 1) * FB, a_cols],
                x[tok_rows, columns(share(p), SL)],
                preferred_element_type=F32,
            ))

    @pl.when(core == 0)
    def _():
        ld_tok.wait()
        normalise(0, TOK)
        pl.semaphore_wait(go, 1)
        for i in range(2):
            token_piece(i, 0).start()
            token_piece(i, 1).start()
        ld_cot.wait()
        ld_wg.wait()
        ld_wd.wait()
        forward(0, TOK, 0)
        activate(act, pl.ds(0, TOK))
        mid_cot.wait_recv()
        mid_nrm.wait_recv()
        forward(TOK, TOK, 0)
        activate(act, pl.ds(TOK, TOK))

        def piece(i, _):
            for kind in (0, 1):
                token_piece(i, kind).wait_recv()
                forwarded(i, kind).start()

            @pl.when(i + 2 < NCH)
            def _():
                for kind in (0, 1):
                    token_piece(i + 2, kind).start()

            forward(2 * TOK + i * CH, CH, i * CH)
            return 0

        lax.fori_loop(0, NCH, piece, 0)
        activate(act, pl.ds(2 * TOK, TOK))

    @pl.when(core == 1)
    def _():
        for p in range(3):
            weight_slice(p).start()
        mid_cot.start()
        ld_tok.wait()
        normalise(TOK, TOK)
        mid_nrm.start()
        for p in range(3):
            weight_slice(p).wait_recv()
            gather(p, 0).start()
        pl.semaphore_signal(go, inc=1, device_id=(beside, df), device_id_type=MESH)
        for p in range(3):
            gather(p, 0).wait_recv()
            gather(p, 1).start()
        ld_cot.wait()
        ld_wg.wait()
        ld_wd.wait()
        for p in range(3):
            gather(p, 1).wait_recv()
            gather(p, 2).start()
        forward(TOK, TOK, 0)
        activate(act, pl.ds(TOK, TOK))

        proj[...] = jnp.zeros_like(proj)

        def partial(r, _):
            for p in range(2):
                j = share_ag(d, p, r)
                cols = pl.ds(pl.multiple_of(j * SL + p * 256, 256), 256)
                proj[:, 0:384] += jnp.dot(nrm[mid, cols], wf[p, r], preferred_element_type=F32)
            proj[:, 384:576] += lax.dot_general(
                ctg[mid, columns(share_ag(d, 2, r), SL)], wfd[r],
                (((1,), (1,)), ((), ())), preferred_element_type=F32,
            )
            return 0

        lax.fori_loop(0, 4, partial, 0)
        for p in range(3):
            gather(p, 2).wait_recv()
        lax.fori_loop(4, 8, partial, 0)
        activate(actf, pl.ds(0, TOK))

        def term(r, put):
            grads(actf, slice(0, TOK), mid, lambda p: flip(share_rs(d, p, r)), put)

        reduce_scatter(term, rcvf, rf_s, rf_r)
        for p in range(3):
            back[p] = acc[p, 0].astype(BF16)
            returned(p).start()

        def piece(i, _):
            for kind in (0, 1):
                forwarded(i, kind).wait_recv()
            forward(2 * TOK + i * CH, CH, i * CH)
            return 0

        lax.fori_loop(0, NCH, piece, 0)
        activate(act, pl.ds(2 * TOK, TOK))

    def own_term(r, put):
        @pl.when(core == 0)
        def _():
            grads(act, slice(0, 3 * TOK), pl.ds(0, 3 * TOK), lambda p: share_rs(d, p, r), put)

        @pl.when(core == 1)
        def _():
            grads(act, slice(TOK, 3 * TOK), pl.ds(TOK, 2 * TOK), lambda p: share_rs(d, p, r), put)

    reduce_scatter(own_term, rcv, rs_s, rs_r)

    @pl.when(core == 1)
    def _():
        for p in range(3):
            returned(p).wait_recv()
            acc[p, 0] = acc[p, 0] + ret[p].astype(F32)

    o_gu[:, 0:FB] = (acc[0, 0] * scale).T
    o_gu[:, FB:2 * FB] = (acc[1, 0] * scale).T
    o_dn[...] = acc[2, 0] * scale

    @pl.when(core == 0)
    def _():
        for i in range(NCH):
            for kind in (0, 1):
                token_piece(i, kind).wait_send()
                forwarded(i, kind).wait_send()

    @pl.when(core == 1)
    def _():
        mid_cot.wait_send()
        mid_nrm.wait_send()
        for p in range(3):
            weight_slice(p).wait_send()
            returned(p).wait_send()
            for step in range(3):
                gather(p, step).wait_send()


def local(tokens, cotangent, gain, gate_up, down):
    scale = 1.0 / math.sqrt(3 * TOK * 8)
    anywhere = pl.BlockSpec(memory_space=pl.ANY)
    vmem = pl.BlockSpec(memory_space=pltpu.VMEM)
    dma = pltpu.SemaphoreType.DMA
    return pl.pallas_call(
        functools.partial(kernel, scale),
        out_shape=(
            jax.ShapeDtypeStruct((SL, 2 * FB), F32),
            jax.ShapeDtypeStruct((FB, SL), F32),
        ),
        in_specs=[anywhere, anywhere, vmem, anywhere, anywhere],
        out_specs=(vmem, vmem),
        scratch_shapes=[
            pltpu.VMEM((3 * TOK, D), BF16),
            pltpu.VMEM((3 * TOK, D), BF16),
            pltpu.VMEM((D, 2 * FB), BF16),
            pltpu.VMEM((FB, D), BF16),
            pltpu.VMEM((2, 8, 256, 2 * FB), BF16),
            pltpu.VMEM((8, FB, SL), BF16),
            pltpu.VMEM((TOK, 3 * FB), F32),
            pltpu.VMEM((3 * FB, 3 * TOK), BF16),
            pltpu.VMEM((3 * FB, TOK), BF16),
            pltpu.VMEM((3, 7, FB, SL), BF16),
            pltpu.VMEM((3, 7, FB, SL), BF16),
            pltpu.VMEM((3, 7, FB, SL), BF16),
            pltpu.VMEM((3, 4, FB, SL), F32),
            pltpu.VMEM((3, FB, SL), BF16),
            pltpu.VMEM((3, FB, SL), BF16),
            dma((4,)),
            dma((3,)), dma((3,)), dma((3, 3)), dma((3, 3)),
            dma((3, 7)), dma((3, 7)), dma((3, 7)), dma((3, 7)),
            dma((NCH, 2)), dma((NCH, 2)), dma((NCH, 2)), dma((NCH, 2)),
            dma((2,)), dma((2,)), dma((3,)), dma((3,)),
            pltpu.SemaphoreType.REGULAR,
        ],
        compiler_params=pltpu.CompilerParams(
            collective_id=0, has_side_effects=True, vmem_limit_bytes=58 << 20
        ),
        name="grads",
    )(tokens, cotangent, gain.reshape(1, D), gate_up, down)


def solution(mesh):
    in_specs = (P(("blk", "dp"), None), P(("blk", "dp"), None), P(), P(None, "blk"), P("blk", None))
    out_specs = (P("dp", "blk"), P("blk", "dp"))
    return jax.shard_map(local, mesh=mesh, in_specs=in_specs, out_specs=out_specs, check_vma=False)
```

```python
import functools
import math

import jax
import jax.numpy as jnp
from jax import lax
from jax.experimental import pallas as pl
from jax.experimental.pallas import tpu as pltpu
from jax.sharding import PartitionSpec as P

MESH = pl.DeviceIdType.MESH
F32 = jnp.float32
BF16 = jnp.bfloat16

TOK = 256
D = 4096
FB = 192
SL = D // 8
CH = 64
NCH = TOK // CH

ORDERS = (("a", "b", "y"), ("b", "y", "a"), ("y", "a", "b"))


def flip(v):
    return v + 1 - 2 * lax.rem(v, 2)


def moved(d, toggle):
    x, y = d // 2, lax.rem(d, 2)
    x = x + toggle["a"] * (1 - 2 * lax.rem(x, 2))
    x = lax.rem(x + toggle["b"] * (2 * lax.rem(x, 2) - 1) + 4, 4)
    y = y + toggle["y"] * (1 - 2 * y)
    return 2 * x + y


def partner(d, dim):
    return moved(d, {name: int(name == dim) for name in "aby"})


def share_rs(d, p, r):
    o = ORDERS[p]
    return moved(d, {o[0]: r // 4, o[1]: lax.rem(r // 2, 2), o[2]: lax.rem(r, 2)})


def share_ag(d, p, r):
    o = ORDERS[p]
    return moved(d, {o[2]: r // 4, o[1]: lax.rem(r // 2, 2), o[0]: lax.rem(r, 2)})


def columns(j, width):
    return pl.ds(pl.multiple_of(j * width, width), width)


def finish(scale, sums, o_gu, o_dn):
    o_gu[:, 0:FB] = (sums[0] * scale).T
    o_gu[:, FB:2 * FB] = (sums[1] * scale).T
    o_dn[...] = sums[2] * scale


def kernel(
    tok, cot, gain, gu, dn,
    out,
    nrm, ctg, wg, wd, wf, wfd, proj, act, actf, snd, rcv, rcvf, acc, back, ret,
    ld_sem, ws_s, ws_r, ag_s, ag_r, rs_s, rs_r, rf_s, rf_r,
    tk_s, tk_r, fw_s, fw_r, t1_s, t1_r, rt_s, rt_r, go,
):
    b = lax.axis_index("blk")
    d = lax.axis_index("dp")
    core = lax.rem(b, 2)
    n_blk = 32
    nxt = lax.rem(b + 2, n_blk)
    prv = lax.rem(b + n_blk - 2, n_blk)
    other = flip(b)
    beside = lax.rem(b + n_blk - 1 + 2 * core, n_blk)
    df = flip(d)
    own = pl.ds(pl.multiple_of(core * TOK, TOK), TOK)

    def load(i, src, dst):
        return pltpu.make_async_copy(src, dst, ld_sem.at[i])

    def remote(src, dst, ss, rs, tb, td):
        return pltpu.make_async_remote_copy(
            src_ref=src, dst_ref=dst, send_sem=ss, recv_sem=rs,
            device_id=(tb, td), device_id_type=MESH,
        )

    ld_tok = load(0, tok, nrm.at[own])
    ld_cot = load(1, cot, ctg.at[own])
    ld_wg = load(2, gu, wg)
    ld_wd = load(3, dn, wd)
    ld_tok.start()

    def load_rest():
        ld_cot.start()
        ld_wg.start()
        ld_wd.start()

    barrier = pltpu.get_barrier_semaphore()
    greeted = [(other, d), (nxt, df), (prv, df), (beside, df)] + [(b, partner(d, k)) for k in "aby"]
    for tb, td in greeted:
        pl.semaphore_signal(barrier, inc=1, device_id=(tb, td), device_id_type=MESH)
    pl.semaphore_wait(barrier, len(greeted))

    def weight_slice(p):
        if p == 2:
            return remote(dn.at[:, columns(df, SL)], wfd.at[0], ws_s.at[2], ws_r.at[2], nxt, df)
        rows = pl.ds(pl.multiple_of(df * SL + p * 256, 256), 256)
        return remote(gu.at[rows, :], wf.at[p, 0], ws_s.at[p], ws_r.at[p], nxt, df)

    def gather(p, src, step):
        ref = wfd if p == 2 else wf.at[p]
        dst = src + 2 ** step
        return remote(
            ref.at[src], ref.at[dst], ag_s.at[p, dst - 1], ag_r.at[p, dst - 1],
            b, partner(d, ORDERS[p][step]),
        )

    gathers = [(0, 0), (0, 1), (0, 2), (1, 1), (1, 2), (2, 2), (3, 2)]

    def token_piece(i, kind):
        here = pl.ds(pl.multiple_of(i * CH, CH), CH)
        there = pl.ds(pl.multiple_of(2 * TOK + i * CH, CH), CH)
        if kind == 0:
            return remote(cot.at[here], ctg.at[there], tk_s.at[i, 0], tk_r.at[i, 0], prv, df)
        return remote(nrm.at[here], nrm.at[there], tk_s.at[i, 1], tk_r.at[i, 1], prv, df)

    def forwarded(i, kind):
        there = pl.ds(pl.multiple_of(2 * TOK + i * CH, CH), CH)
        ref = nrm if kind else ctg
        return remote(ref.at[there], ref.at[there], fw_s.at[i, kind], fw_r.at[i, kind], other, d)

    mid = pl.ds(TOK, TOK)
    mid_cot = remote(cot, ctg.at[mid], t1_s.at[0], t1_r.at[0], other, d)
    mid_nrm = remote(nrm.at[mid], nrm.at[mid], t1_s.at[1], t1_r.at[1], other, d)

    def returned(p):
        return remote(back.at[p], ret.at[p], rt_s.at[p], rt_r.at[p], prv, df)

    def normalise(row0, n):
        def body(i, _):
            rows = pl.ds(pl.multiple_of(row0 + i * 16, 16), 16)
            v = nrm[rows, :].astype(F32)
            inv = lax.rsqrt(jnp.mean(v * v, axis=-1, keepdims=True) + 1e-06)
            nrm[rows, :] = (v * inv * gain[...]).astype(BF16)
            return 0

        lax.fori_loop(0, n // 16, body, 0)

    def forward(row0, n, to):
        rows = pl.ds(pl.multiple_of(row0, CH), n)
        out = pl.ds(pl.multiple_of(to, CH), n)
        proj[out, 0:384] = jnp.dot(nrm[rows, :], wg[...], preferred_element_type=F32)
        proj[out, 384:576] = lax.dot_general(
            ctg[rows, :], wd[...], (((1,), (1,)), ((), ())), preferred_element_type=F32
        )

    def activate(dst, cols):
        t = proj[...].T
        gate, up, bk = t[0:FB], t[FB:2 * FB], t[2 * FB:3 * FB]
        s = jax.nn.sigmoid(gate)
        dst[0:FB, cols] = (bk * up * (s * (1.0 + gate * (1.0 - s)))).astype(BF16)
        dst[FB:2 * FB, cols] = (bk * gate * s).astype(BF16)
        dst[2 * FB:3 * FB, cols] = (gate * s * up).astype(BF16)

    def reduce_scatter(term, r_ref, s_sem, r_sem, beside_it=None):
        def copy(p, slot, step):
            return remote(
                snd.at[p, slot], r_ref.at[p, slot], s_sem.at[p, slot], r_sem.at[p, slot],
                b, partner(d, ORDERS[p][step]),
            )

        def first(i, _):
            q = 3 - 2 * lax.rem(i, 2) - i // 2

            def put(p, v):
                snd[p, q] = v.astype(BF16)

            term(q + 4, put)
            for p in range(3):
                copy(p, q, 0).start()
            return 0

        def kept(i, _):
            q = 3 - 2 * lax.rem(i, 2) - i // 2

            def put(p, v):
                acc[p, q] = v

            term(q, put)
            return 0

        lax.fori_loop(0, 4, first, 0)
        lax.fori_loop(0, 4, kept, 0)
        if beside_it is not None:
            beside_it(0)
        for q in (3, 1, 2, 0):
            for p in range(3):
                copy(p, q, 0).wait_recv()
                v = acc[p, q] + r_ref[p, q].astype(F32)
                if q >= 2:
                    snd[p, q + 2] = v.astype(BF16)
                    copy(p, q + 2, 1).start()
                else:
                    acc[p, q] = v
        if beside_it is not None:
            beside_it(1)
        for p in range(3):
            copy(p, 5, 1).wait_recv()
            snd[p, 6] = (acc[p, 1] + r_ref[p, 5].astype(F32)).astype(BF16)
            copy(p, 6, 2).start()
        for p in range(3):
            copy(p, 4, 1).wait_recv()
            acc[p, 0] = acc[p, 0] + r_ref[p, 4].astype(F32)
        for p in range(3):
            copy(p, 6, 2).wait_recv()
            acc[p, 0] = acc[p, 0] + r_ref[p, 6].astype(F32)
        for p in range(3):
            for slot, step in [(k, 0) for k in range(4)] + [(4, 1), (5, 1), (6, 2)]:
                copy(p, slot, step).wait_send()

    def grads(a_ref, a_cols, tok_rows, share, put):
        for p in range(3):
            x = ctg if p == 2 else nrm
            put(p, jnp.dot(
                a_ref[p * FB:(p + 1) * FB, a_cols],
                x[tok_rows, columns(share(p), SL)],
                preferred_element_type=F32,
            ))

    @pl.when(core == 0)
    def _():
        load_rest()
        ld_tok.wait()
        normalise(0, TOK)
        pl.semaphore_wait(go, 1)
        for i in range(NCH):
            token_piece(i, 0).start()
            token_piece(i, 1).start()
        ld_cot.wait()
        ld_wg.wait()
        ld_wd.wait()
        forward(0, TOK, 0)
        activate(act, pl.ds(0, TOK))
        mid_cot.wait_recv()
        mid_nrm.wait_recv()
        forward(TOK, TOK, 0)
        activate(act, pl.ds(TOK, TOK))

        def piece(i, _):
            for kind in (0, 1):
                token_piece(i, kind).wait_recv()
                forwarded(i, kind).start()

            forward(2 * TOK + i * CH, CH, i * CH)
            return 0

        lax.fori_loop(0, NCH, piece, 0)
        activate(act, pl.ds(2 * TOK, TOK))

    @pl.when(core == 1)
    def _():
        for p in range(3):
            weight_slice(p).start()
        mid_cot.start()
        load_rest()
        ld_tok.wait()
        normalise(TOK, TOK)
        mid_nrm.start()
        for p in range(3):
            weight_slice(p).wait_recv()
            for step in range(3):
                gather(p, 0, step).start()
            if p == 1:
                pl.semaphore_signal(go, inc=1, device_id=(beside, df), device_id_type=MESH)
        ld_cot.wait()
        ld_wg.wait()
        ld_wd.wait()
        for p in range(3):
            gather(p, 0, 0).wait_recv()
            gather(p, 1, 1).start()
            gather(p, 1, 2).start()
        for p in range(3):
            gather(p, 0, 1).wait_recv()
            gather(p, 2, 2).start()
        forward(TOK, TOK, 0)
        activate(act, pl.ds(TOK, TOK))
        for p in range(3):
            gather(p, 1, 1).wait_recv()
            gather(p, 3, 2).start()

        proj[...] = jnp.zeros_like(proj)

        def partial(r, _):
            for p in range(2):
                j = share_ag(d, p, r)
                cols = pl.ds(pl.multiple_of(j * SL + p * 256, 256), 256)
                proj[:, 0:384] += jnp.dot(nrm[mid, cols], wf[p, r], preferred_element_type=F32)
            proj[:, 384:576] += lax.dot_general(
                ctg[mid, columns(share_ag(d, 2, r), SL)], wfd[r],
                (((1,), (1,)), ((), ())), preferred_element_type=F32,
            )
            return 0

        lax.fori_loop(0, 4, partial, 0)
        for src in range(4):
            for p in range(3):
                gather(p, src, 2).wait_recv()
            partial(src + 4, 0)
        activate(actf, pl.ds(0, TOK))

        def term(r, put):
            grads(actf, slice(0, TOK), mid, lambda p: flip(share_rs(d, p, r)), put)

        def piece(i):
            for kind in (0, 1):
                forwarded(i, kind).wait_recv()
            forward(2 * TOK + i * CH, CH, i * CH)

        reduce_scatter(term, rcvf, rf_s, rf_r, piece)
        for p in range(3):
            back[p] = acc[p, 0].astype(BF16)
        for i in range(2, NCH):
            piece(i)
        activate(act, pl.ds(2 * TOK, TOK))
        for p in range(3):
            returned(p).start()

    def own_term(r, put):
        @pl.when(core == 0)
        def _():
            grads(act, slice(0, 3 * TOK), pl.ds(0, 3 * TOK), lambda p: share_rs(d, p, r), put)

        @pl.when(core == 1)
        def _():
            grads(act, slice(TOK, 3 * TOK), pl.ds(TOK, 2 * TOK), lambda p: share_rs(d, p, r), put)

    reduce_scatter(own_term, rcv, rs_s, rs_r)

    @pl.when(core == 1)
    def _():
        for p in range(3):
            returned(p).wait_recv()
            acc[p, 0] = acc[p, 0] + ret[p].astype(F32)

    for p in range(3):
        out[p] = acc[p, 0]

    @pl.when(core == 0)
    def _():
        for i in range(NCH):
            for kind in (0, 1):
                token_piece(i, kind).wait_send()
                forwarded(i, kind).wait_send()

    @pl.when(core == 1)
    def _():
        mid_cot.wait_send()
        mid_nrm.wait_send()
        for p in range(3):
            weight_slice(p).wait_send()
            returned(p).wait_send()
            for src, step in gathers:
                gather(p, src, step).wait_send()


def local(tokens, cotangent, gain, gate_up, down):
    scale = 1.0 / math.sqrt(3 * TOK * 8)
    anywhere = pl.BlockSpec(memory_space=pl.ANY)
    vmem = pl.BlockSpec(memory_space=pltpu.VMEM)
    dma = pltpu.SemaphoreType.DMA
    sums = pl.pallas_call(
        kernel,
        out_shape=jax.ShapeDtypeStruct((3, FB, SL), F32),
        in_specs=[anywhere, anywhere, vmem, anywhere, anywhere],
        out_specs=vmem,
        scratch_shapes=[
            pltpu.VMEM((3 * TOK, D), BF16),
            pltpu.VMEM((3 * TOK, D), BF16),
            pltpu.VMEM((D, 2 * FB), BF16),
            pltpu.VMEM((FB, D), BF16),
            pltpu.VMEM((2, 8, 256, 2 * FB), BF16),
            pltpu.VMEM((8, FB, SL), BF16),
            pltpu.VMEM((TOK, 3 * FB), F32),
            pltpu.VMEM((3 * FB, 3 * TOK), BF16),
            pltpu.VMEM((3 * FB, TOK), BF16),
            pltpu.VMEM((3, 7, FB, SL), BF16),
            pltpu.VMEM((3, 7, FB, SL), BF16),
            pltpu.VMEM((3, 7, FB, SL), BF16),
            pltpu.VMEM((3, 4, FB, SL), F32),
            pltpu.VMEM((3, FB, SL), BF16),
            pltpu.VMEM((3, FB, SL), BF16),
            dma((4,)),
            dma((3,)), dma((3,)), dma((3, 7)), dma((3, 7)),
            dma((3, 7)), dma((3, 7)), dma((3, 7)), dma((3, 7)),
            dma((NCH, 2)), dma((NCH, 2)), dma((NCH, 2)), dma((NCH, 2)),
            dma((2,)), dma((2,)), dma((3,)), dma((3,)),
            pltpu.SemaphoreType.REGULAR,
        ],
        compiler_params=pltpu.CompilerParams(
            collective_id=0, has_side_effects=True, vmem_limit_bytes=58 << 20
        ),
        name="grads",
    )(tokens, cotangent, gain.reshape(1, D), gate_up, down)
    return pl.pallas_call(
        functools.partial(finish, scale),
        out_shape=(
            jax.ShapeDtypeStruct((SL, 2 * FB), F32),
            jax.ShapeDtypeStruct((FB, SL), F32),
        ),
        in_specs=[vmem],
        out_specs=(vmem, vmem),
        name="scaled",
    )(sums)


def solution(mesh):
    in_specs = (P(("blk", "dp"), None), P(("blk", "dp"), None), P(), P(None, "blk"), P("blk", None))
    out_specs = (P("dp", "blk"), P("blk", "dp"))
    return jax.shard_map(local, mesh=mesh, in_specs=in_specs, out_specs=out_specs, check_vma=False)
```

```python
import functools
import math

import jax
import jax.numpy as jnp
from jax import lax
from jax.experimental import pallas as pl
from jax.experimental.pallas import tpu as pltpu
from jax.sharding import PartitionSpec as P

MESH = pl.DeviceIdType.MESH
F32 = jnp.float32
BF16 = jnp.bfloat16

TOK = 256
D = 4096
FB = 192
SL = D // 8
CH = 64
NCH = TOK // CH

ORDERS = (("a", "b", "y"), ("b", "y", "a"), ("y", "a", "b"))


def flip(v):
    return v + 1 - 2 * lax.rem(v, 2)


def moved(d, toggle):
    x, y = d // 2, lax.rem(d, 2)
    x = x + toggle["a"] * (1 - 2 * lax.rem(x, 2))
    x = lax.rem(x + toggle["b"] * (2 * lax.rem(x, 2) - 1) + 4, 4)
    y = y + toggle["y"] * (1 - 2 * y)
    return 2 * x + y


def partner(d, dim):
    return moved(d, {name: int(name == dim) for name in "aby"})


def share_rs(d, p, r):
    o = ORDERS[p]
    return moved(d, {o[0]: r // 4, o[1]: lax.rem(r // 2, 2), o[2]: lax.rem(r, 2)})


def share_ag(d, p, r):
    o = ORDERS[p]
    return moved(d, {o[2]: r // 4, o[1]: lax.rem(r // 2, 2), o[0]: lax.rem(r, 2)})


def columns(j, width):
    return pl.ds(pl.multiple_of(j * width, width), width)


def finish(scale, sums, o_gu, o_dn):
    o_gu[:, 0:FB] = (sums[0] * scale).T
    o_gu[:, FB:2 * FB] = (sums[1] * scale).T
    o_dn[...] = sums[2] * scale


def kernel(
    tok, cot, gain, gu, dn,
    out,
    nrm, ctg, wg, wd, wf, wfd, proj, act, actf, snd, rcv, rcvf, acc, back, ret,
    ld_sem, ws_s, ws_r, ag_s, ag_r, rs_s, rs_r, rf_s, rf_r,
    tk_s, tk_r, in_s, in_r, rt_s, rt_r, go, done,
):
    b = lax.axis_index("blk")
    d = lax.axis_index("dp")
    core = lax.rem(b, 2)
    n_blk = 32
    nxt = lax.rem(b + 2, n_blk)
    prv = lax.rem(b + n_blk - 2, n_blk)
    other = flip(b)
    beside = lax.rem(b + n_blk - 1 + 2 * core, n_blk)
    df = flip(d)
    own = pl.ds(pl.multiple_of(core * TOK, TOK), TOK)

    def load(i, src, dst):
        return pltpu.make_async_copy(src, dst, ld_sem.at[i])

    def remote(src, dst, ss, rs, tb, td):
        return pltpu.make_async_remote_copy(
            src_ref=src, dst_ref=dst, send_sem=ss, recv_sem=rs,
            device_id=(tb, td), device_id_type=MESH,
        )

    ld_tok = load(0, tok, nrm.at[own])
    ld_cot = load(1, cot, ctg.at[own])
    ld_wg = load(2, gu, wg)
    ld_wd = load(3, dn, wd)
    ld_tok.start()

    def load_rest():
        ld_cot.start()
        ld_wg.start()
        ld_wd.start()

    barrier = pltpu.get_barrier_semaphore()
    greeted = [(other, d), (nxt, df), (prv, df), (beside, df)] + [(b, partner(d, k)) for k in "aby"]
    for tb, td in greeted:
        pl.semaphore_signal(barrier, inc=1, device_id=(tb, td), device_id_type=MESH)
    pl.semaphore_wait(barrier, len(greeted))

    def weight_slice(p):
        if p == 2:
            return remote(dn.at[:, columns(df, SL)], wfd.at[0], ws_s.at[2], ws_r.at[2], nxt, df)
        rows = pl.ds(pl.multiple_of(df * SL + p * 256, 256), 256)
        return remote(gu.at[rows, :], wf.at[p, 0], ws_s.at[p], ws_r.at[p], nxt, df)

    def gather(p, src, step):
        ref = wfd if p == 2 else wf.at[p]
        dst = src + 2 ** step
        return remote(
            ref.at[src], ref.at[dst], ag_s.at[p, dst - 1], ag_r.at[p, dst - 1],
            b, partner(d, ORDERS[p][step]),
        )

    gathers = [(0, 0), (0, 1), (0, 2), (1, 1), (1, 2), (2, 2), (3, 2)]

    def token_piece(i, kind):
        here = pl.ds(pl.multiple_of(i * CH, CH), CH)
        there = pl.ds(pl.multiple_of(2 * TOK + i * CH, CH), CH)
        if kind == 0:
            return remote(cot.at[here], ctg.at[there], tk_s.at[i, 0], tk_r.at[i, 0], prv, df)
        return remote(nrm.at[here], nrm.at[there], tk_s.at[i, 1], tk_r.at[i, 1], prv, df)

    low, mid = pl.ds(0, TOK), pl.ds(TOK, TOK)
    low_cot = remote(cot, ctg.at[low], in_s.at[0], in_r.at[0], other, d)
    low_nrm = remote(nrm.at[low], nrm.at[low], in_s.at[1], in_r.at[1], other, d)
    mid_cot = remote(cot, ctg.at[mid], in_s.at[2], in_r.at[2], other, d)
    mid_nrm = remote(nrm.at[mid], nrm.at[mid], in_s.at[3], in_r.at[3], other, d)

    def returned(p):
        return remote(back.at[p], ret.at[p], rt_s.at[p], rt_r.at[p], prv, df)

    def normalise(row0, n):
        def body(i, _):
            rows = pl.ds(pl.multiple_of(row0 + i * 16, 16), 16)
            v = nrm[rows, :].astype(F32)
            inv = lax.rsqrt(jnp.mean(v * v, axis=-1, keepdims=True) + 1e-06)
            nrm[rows, :] = (v * inv * gain[...]).astype(BF16)
            return 0

        lax.fori_loop(0, n // 16, body, 0)

    def forward(row0, n, to):
        rows = pl.ds(pl.multiple_of(row0, CH), n)
        out = pl.ds(pl.multiple_of(to, CH), n)
        proj[out, 0:384] = jnp.dot(nrm[rows, :], wg[...], preferred_element_type=F32)
        proj[out, 384:576] = lax.dot_general(
            ctg[rows, :], wd[...], (((1,), (1,)), ((), ())), preferred_element_type=F32
        )

    def activate(dst, col, n):
        cols = slice(col, col + n)
        t = proj[0:n].T
        gate, up, bk = t[0:FB], t[FB:2 * FB], t[2 * FB:3 * FB]
        s = jax.nn.sigmoid(gate)
        dst[0:FB, cols] = (bk * up * (s * (1.0 + gate * (1.0 - s)))).astype(BF16)
        dst[FB:2 * FB, cols] = (bk * gate * s).astype(BF16)
        dst[2 * FB:3 * FB, cols] = (gate * s * up).astype(BF16)

    def reduce_scatter(term, r_ref, s_sem, r_sem, beside_it=lambda k: None):
        def copy(p, slot, step):
            return remote(
                snd.at[p, slot], r_ref.at[p, slot], s_sem.at[p, slot], r_sem.at[p, slot],
                b, partner(d, ORDERS[p][step]),
            )

        def first(i, _):
            q = 3 - 2 * lax.rem(i, 2) - i // 2

            def put(p, v):
                snd[p, q] = v.astype(BF16)

            term(q + 4, put)
            for p in range(3):
                copy(p, q, 0).start()
            return 0

        def kept(i, _):
            q = 3 - 2 * lax.rem(i, 2) - i // 2

            def put(p, v):
                acc[p, q] = v

            term(q, put)
            return 0

        lax.fori_loop(0, 4, first, 0)
        beside_it(0)
        lax.fori_loop(0, 4, kept, 0)
        for q in (3, 1, 2, 0):
            for p in range(3):
                copy(p, q, 0).wait_recv()
                v = acc[p, q] + r_ref[p, q].astype(F32)
                if q >= 2:
                    snd[p, q + 2] = v.astype(BF16)
                    copy(p, q + 2, 1).start()
                else:
                    acc[p, q] = v
        beside_it(1)
        for p in range(3):
            copy(p, 5, 1).wait_recv()
            snd[p, 6] = (acc[p, 1] + r_ref[p, 5].astype(F32)).astype(BF16)
            copy(p, 6, 2).start()
        beside_it(2)
        for p in range(3):
            copy(p, 4, 1).wait_recv()
            acc[p, 0] = acc[p, 0] + r_ref[p, 4].astype(F32)
        for p in range(3):
            copy(p, 6, 2).wait_recv()
            acc[p, 0] = acc[p, 0] + r_ref[p, 6].astype(F32)
        beside_it(3)
        for p in range(3):
            for slot, step in [(k, 0) for k in range(4)] + [(4, 1), (5, 1), (6, 2)]:
                copy(p, slot, step).wait_send()

    def grads(a_ref, a_cols, tok_rows, share, put):
        for p in range(3):
            x = ctg if p == 2 else nrm
            put(p, jnp.dot(
                a_ref[p * FB:(p + 1) * FB, a_cols],
                x[tok_rows, columns(share(p), SL)],
                preferred_element_type=F32,
            ))

    @pl.when(core == 0)
    def _():
        low_cot.start()
        load_rest()
        ld_tok.wait()
        normalise(0, TOK)
        low_nrm.start()
        pl.semaphore_wait(go, 1)
        for i in range(NCH):
            token_piece(i, 0).start()
            token_piece(i, 1).start()
        ld_cot.wait()
        ld_wg.wait()
        ld_wd.wait()
        forward(0, TOK, 0)
        activate(act, 0, TOK)
        mid_cot.wait_recv()
        mid_nrm.wait_recv()
        forward(TOK, TOK, 0)
        activate(act, TOK, TOK)

        def piece(i, _):
            for kind in (0, 1):
                token_piece(i, kind).wait_recv()
            forward(2 * TOK + i * CH, CH, i * CH)
            return 0

        lax.fori_loop(0, NCH, piece, 0)
        pl.semaphore_signal(done, inc=1, device_id=(other, d), device_id_type=MESH)
        activate(act, 2 * TOK, TOK)

        def term(r, put):
            grads(act, slice(0, 3 * TOK), pl.ds(0, 3 * TOK), lambda p: share_rs(d, p, r), put)

        reduce_scatter(term, rcv, rs_s, rs_r)
        for p in range(3):
            out[p] = acc[p, 0]
        low_cot.wait_send()
        low_nrm.wait_send()
        for i in range(NCH):
            for kind in (0, 1):
                token_piece(i, kind).wait_send()

    @pl.when(core == 1)
    def _():
        for p in range(3):
            weight_slice(p).start()
        mid_cot.start()
        load_rest()
        ld_tok.wait()
        normalise(TOK, TOK)
        mid_nrm.start()
        ld_cot.wait()
        ld_wg.wait()
        ld_wd.wait()
        forward(TOK, TOK, 0)
        activate(act, TOK, TOK)

        def term(r, put):
            grads(act, slice(TOK, 2 * TOK), mid, lambda p: share_rs(d, p, r), put)

        def gathering(k):
            for p in range(3):
                if k == 0:
                    weight_slice(p).wait_recv()
                    for step in range(3):
                        gather(p, 0, step).start()
                    if p == 1:
                        pl.semaphore_signal(
                            go, inc=1, device_id=(beside, df), device_id_type=MESH
                        )
                elif k == 1:
                    gather(p, 0, 0).wait_recv()
                    gather(p, 1, 1).start()
                    gather(p, 1, 2).start()
                elif k == 2:
                    gather(p, 0, 1).wait_recv()
                    gather(p, 2, 2).start()
                else:
                    gather(p, 1, 1).wait_recv()
                    gather(p, 3, 2).start()

        reduce_scatter(term, rcv, rs_s, rs_r, gathering)
        for p in range(3):
            out[p] = acc[p, 0]

        proj[...] = jnp.zeros_like(proj)
        both = pl.ds(0, 2 * TOK)
        low_cot.wait_recv()
        low_nrm.wait_recv()

        def partial(r, _):
            for p in range(2):
                j = share_ag(d, p, r)
                cols = pl.ds(pl.multiple_of(j * SL + p * 256, 256), 256)
                proj[:, 0:384] += jnp.dot(nrm[both, cols], wf[p, r], preferred_element_type=F32)
            proj[:, 384:576] += lax.dot_general(
                ctg[both, columns(share_ag(d, 2, r), SL)], wfd[r],
                (((1,), (1,)), ((), ())), preferred_element_type=F32,
            )
            return 0

        lax.fori_loop(0, 4, partial, 0)
        for src in range(4):
            for p in range(3):
                gather(p, src, 2).wait_recv()
            partial(src + 4, 0)
        activate(actf, 0, 2 * TOK)

        def foreign(r, put):
            grads(actf, slice(0, 2 * TOK), both, lambda p: flip(share_rs(d, p, r)), put)

        reduce_scatter(foreign, rcvf, rf_s, rf_r)
        for p in range(3):
            back[p] = acc[p, 0].astype(BF16)
        pl.semaphore_wait(done, 1)
        for p in range(3):
            returned(p).start()
        for p in range(3):
            returned(p).wait_recv()
            out[p] = out[p] + ret[p].astype(F32)

        mid_cot.wait_send()
        mid_nrm.wait_send()
        for p in range(3):
            weight_slice(p).wait_send()
            returned(p).wait_send()
            for src, step in gathers:
                gather(p, src, step).wait_send()


def local(tokens, cotangent, gain, gate_up, down):
    scale = 1.0 / math.sqrt(3 * TOK * 8)
    anywhere = pl.BlockSpec(memory_space=pl.ANY)
    vmem = pl.BlockSpec(memory_space=pltpu.VMEM)
    dma = pltpu.SemaphoreType.DMA
    sums = pl.pallas_call(
        kernel,
        out_shape=jax.ShapeDtypeStruct((3, FB, SL), F32),
        in_specs=[anywhere, anywhere, vmem, anywhere, anywhere],
        out_specs=vmem,
        scratch_shapes=[
            pltpu.VMEM((3 * TOK, D), BF16),
            pltpu.VMEM((3 * TOK, D), BF16),
            pltpu.VMEM((D, 2 * FB), BF16),
            pltpu.VMEM((FB, D), BF16),
            pltpu.VMEM((2, 8, 256, 2 * FB), BF16),
            pltpu.VMEM((8, FB, SL), BF16),
            pltpu.VMEM((2 * TOK, 3 * FB), F32),
            pltpu.VMEM((3 * FB, 3 * TOK), BF16),
            pltpu.VMEM((3 * FB, 2 * TOK), BF16),
            pltpu.VMEM((3, 7, FB, SL), BF16),
            pltpu.VMEM((3, 7, FB, SL), BF16),
            pltpu.VMEM((3, 7, FB, SL), BF16),
            pltpu.VMEM((3, 4, FB, SL), F32),
            pltpu.VMEM((3, FB, SL), BF16),
            pltpu.VMEM((3, FB, SL), BF16),
            dma((4,)),
            dma((3,)), dma((3,)), dma((3, 7)), dma((3, 7)),
            dma((3, 7)), dma((3, 7)), dma((3, 7)), dma((3, 7)),
            dma((NCH, 2)), dma((NCH, 2)), dma((4,)), dma((4,)), dma((3,)), dma((3,)),
            pltpu.SemaphoreType.REGULAR, pltpu.SemaphoreType.REGULAR,
        ],
        compiler_params=pltpu.CompilerParams(
            collective_id=0, has_side_effects=True, vmem_limit_bytes=58 << 20
        ),
        name="grads",
    )(tokens, cotangent, gain.reshape(1, D), gate_up, down)
    return pl.pallas_call(
        functools.partial(finish, scale),
        out_shape=(
            jax.ShapeDtypeStruct((SL, 2 * FB), F32),
            jax.ShapeDtypeStruct((FB, SL), F32),
        ),
        in_specs=[vmem],
        out_specs=(vmem, vmem),
        name="scaled",
    )(sums)


def solution(mesh):
    in_specs = (P(("blk", "dp"), None), P(("blk", "dp"), None), P(), P(None, "blk"), P("blk", None))
    out_specs = (P("dp", "blk"), P("blk", "dp"))
    return jax.shard_map(local, mesh=mesh, in_specs=in_specs, out_specs=out_specs, check_vma=False)
```

```python
import functools
import math

import jax
import jax.numpy as jnp
from jax import lax
from jax.experimental import pallas as pl
from jax.experimental.pallas import tpu as pltpu
from jax.sharding import PartitionSpec as P

MESH = pl.DeviceIdType.MESH
F32 = jnp.float32
BF16 = jnp.bfloat16

TOK = 256
D = 4096
FB = 192
SL = D // 8
CH = 64
NCH = TOK // CH

ORDERS = (("a", "b", "y"), ("b", "y", "a"), ("y", "a", "b"))


def flip(v):
    return v + 1 - 2 * lax.rem(v, 2)


def moved(d, toggle):
    x, y = d // 2, lax.rem(d, 2)
    x = x + toggle["a"] * (1 - 2 * lax.rem(x, 2))
    x = lax.rem(x + toggle["b"] * (2 * lax.rem(x, 2) - 1) + 4, 4)
    y = y + toggle["y"] * (1 - 2 * y)
    return 2 * x + y


def partner(d, dim):
    return moved(d, {name: int(name == dim) for name in "aby"})


def share_rs(d, p, r):
    o = ORDERS[p]
    return moved(d, {o[0]: r // 4, o[1]: lax.rem(r // 2, 2), o[2]: lax.rem(r, 2)})


def share_ag(d, p, r):
    o = ORDERS[p]
    return moved(d, {o[2]: r // 4, o[1]: lax.rem(r // 2, 2), o[0]: lax.rem(r, 2)})


def columns(j, width):
    return pl.ds(pl.multiple_of(j * width, width), width)


def finish(scale, sums, o_gu, o_dn):
    o_gu[:, 0:FB] = (sums[0] * scale).T
    o_gu[:, FB:2 * FB] = (sums[1] * scale).T
    o_dn[...] = sums[2] * scale


def kernel(
    tok, cot, gain, gu, dn,
    out,
    nrm, ctg, wg, wd, wf, wfd, proj, act, actf, snd, rcv, rcvf, acc, back, ret,
    ld_sem, ws_s, ws_r, ag_s, ag_r, rs_s, rs_r, rf_s, rf_r,
    tk_s, tk_r, in_s, in_r, rt_s, rt_r, go, done,
):
    b = lax.axis_index("blk")
    d = lax.axis_index("dp")
    core = lax.rem(b, 2)
    n_blk = 32
    nxt = lax.rem(b + 2, n_blk)
    prv = lax.rem(b + n_blk - 2, n_blk)
    other = flip(b)
    beside = lax.rem(b + n_blk - 1 + 2 * core, n_blk)
    df = flip(d)
    own = pl.ds(pl.multiple_of(core * TOK, TOK), TOK)

    def load(i, src, dst):
        return pltpu.make_async_copy(src, dst, ld_sem.at[i])

    def remote(src, dst, ss, rs, tb, td):
        return pltpu.make_async_remote_copy(
            src_ref=src, dst_ref=dst, send_sem=ss, recv_sem=rs,
            device_id=(tb, td), device_id_type=MESH,
        )

    ld_tok = load(0, tok, nrm.at[own])
    ld_cot = load(1, cot, ctg.at[own])
    ld_wg = load(2, gu, wg)
    ld_wd = load(3, dn, wd)
    ld_tok.start()

    def load_rest():
        ld_cot.start()
        ld_wg.start()
        ld_wd.start()

    barrier = pltpu.get_barrier_semaphore()
    greeted = [(other, d), (nxt, df), (prv, df), (beside, df)] + [(b, partner(d, k)) for k in "aby"]
    for tb, td in greeted:
        pl.semaphore_signal(barrier, inc=1, device_id=(tb, td), device_id_type=MESH)
    pl.semaphore_wait(barrier, len(greeted))

    def weight_slice(p):
        if p == 2:
            return remote(dn.at[:, columns(df, SL)], wfd.at[0], ws_s.at[2], ws_r.at[2], nxt, df)
        rows = pl.ds(pl.multiple_of(df * SL + p * 256, 256), 256)
        return remote(gu.at[rows, :], wf.at[p, 0], ws_s.at[p], ws_r.at[p], nxt, df)

    def gather(p, src, step):
        ref = wfd if p == 2 else wf.at[p]
        dst = src + 2 ** step
        return remote(
            ref.at[src], ref.at[dst], ag_s.at[p, dst - 1], ag_r.at[p, dst - 1],
            b, partner(d, ORDERS[p][step]),
        )

    gathers = [(0, 0), (0, 1), (0, 2), (1, 1), (1, 2), (2, 2), (3, 2)]

    def token_piece(i, kind):
        here = pl.ds(pl.multiple_of(i * CH, CH), CH)
        there = pl.ds(pl.multiple_of(2 * TOK + i * CH, CH), CH)
        if kind == 0:
            return remote(cot.at[here], ctg.at[there], tk_s.at[i, 0], tk_r.at[i, 0], prv, df)
        return remote(nrm.at[here], nrm.at[there], tk_s.at[i, 1], tk_r.at[i, 1], prv, df)

    low, mid = pl.ds(0, TOK), pl.ds(TOK, TOK)
    low_cot = remote(cot, ctg.at[low], in_s.at[0], in_r.at[0], other, d)
    low_nrm = remote(nrm.at[low], nrm.at[low], in_s.at[1], in_r.at[1], other, d)
    mid_cot = remote(cot, ctg.at[mid], in_s.at[2], in_r.at[2], other, d)
    mid_nrm = remote(nrm.at[mid], nrm.at[mid], in_s.at[3], in_r.at[3], other, d)

    def returned(p):
        return remote(back.at[p], ret.at[p], rt_s.at[p], rt_r.at[p], prv, df)

    def normalise(row0, n):
        def body(i, _):
            rows = pl.ds(pl.multiple_of(row0 + i * 16, 16), 16)
            v = nrm[rows, :].astype(F32)
            inv = lax.rsqrt(jnp.mean(v * v, axis=-1, keepdims=True) + 1e-06)
            nrm[rows, :] = (v * inv * gain[...]).astype(BF16)
            return 0

        lax.fori_loop(0, n // 16, body, 0)

    def half_forward(row0, n, to, kind):
        rows = pl.ds(pl.multiple_of(row0, CH), n)
        dst = pl.ds(pl.multiple_of(to, CH), n)
        if kind:
            proj[dst, 0:384] = jnp.dot(nrm[rows, :], wg[...], preferred_element_type=F32)
        else:
            proj[dst, 384:576] = lax.dot_general(
                ctg[rows, :], wd[...], (((1,), (1,)), ((), ())), preferred_element_type=F32
            )

    def forward(row0, n, to):
        half_forward(row0, n, to, 0)
        half_forward(row0, n, to, 1)

    def activate(dst, col, n):
        cols = slice(col, col + n)
        t = proj[0:n].T
        gate, up, bk = t[0:FB], t[FB:2 * FB], t[2 * FB:3 * FB]
        s = jax.nn.sigmoid(gate)
        dst[0:FB, cols] = (bk * up * (s * (1.0 + gate * (1.0 - s)))).astype(BF16)
        dst[FB:2 * FB, cols] = (bk * gate * s).astype(BF16)
        dst[2 * FB:3 * FB, cols] = (gate * s * up).astype(BF16)

    def reduce_scatter(term, r_ref, s_sem, r_sem, beside_it=lambda k: None):
        def copy(p, slot, step):
            return remote(
                snd.at[p, slot], r_ref.at[p, slot], s_sem.at[p, slot], r_sem.at[p, slot],
                b, partner(d, ORDERS[p][step]),
            )

        def first(i, _):
            q = 3 - 2 * lax.rem(i, 2) - i // 2

            def put(p, v):
                snd[p, q] = v.astype(BF16)

            term(q + 4, put)
            for p in range(3):
                copy(p, q, 0).start()
            return 0

        def kept(i, _):
            q = 3 - 2 * lax.rem(i, 2) - i // 2

            def put(p, v):
                acc[p, q] = v

            term(q, put)
            return 0

        lax.fori_loop(0, 4, first, 0)
        beside_it(0)
        lax.fori_loop(0, 4, kept, 0)
        for q in (3, 1, 2, 0):
            for p in range(3):
                copy(p, q, 0).wait_recv()
                v = acc[p, q] + r_ref[p, q].astype(F32)
                if q >= 2:
                    snd[p, q + 2] = v.astype(BF16)
                    copy(p, q + 2, 1).start()
                else:
                    acc[p, q] = v
        beside_it(1)
        for p in range(3):
            copy(p, 5, 1).wait_recv()
            snd[p, 6] = (acc[p, 1] + r_ref[p, 5].astype(F32)).astype(BF16)
            copy(p, 6, 2).start()
        beside_it(2)
        for p in range(3):
            copy(p, 4, 1).wait_recv()
            acc[p, 0] = acc[p, 0] + r_ref[p, 4].astype(F32)
        for p in range(3):
            copy(p, 6, 2).wait_recv()
            acc[p, 0] = acc[p, 0] + r_ref[p, 6].astype(F32)
        beside_it(3)
        for p in range(3):
            for slot, step in [(k, 0) for k in range(4)] + [(4, 1), (5, 1), (6, 2)]:
                copy(p, slot, step).wait_send()

    def grads(a_ref, a_cols, tok_rows, share, put):
        for p in range(3):
            x = ctg if p == 2 else nrm
            put(p, jnp.dot(
                a_ref[p * FB:(p + 1) * FB, a_cols],
                x[tok_rows, columns(share(p), SL)],
                preferred_element_type=F32,
            ))

    @pl.when(core == 0)
    def _():
        low_cot.start()
        load_rest()
        ld_tok.wait()
        normalise(0, TOK)
        low_nrm.start()
        pl.semaphore_wait(go, 1)
        for i in range(NCH):
            token_piece(i, 0).start()
            token_piece(i, 1).start()
        ld_cot.wait()
        ld_wg.wait()
        ld_wd.wait()
        forward(0, TOK, 0)
        activate(act, 0, TOK)
        mid_cot.wait_recv()
        mid_nrm.wait_recv()
        forward(TOK, TOK, 0)
        activate(act, TOK, TOK)

        def piece(i, _):
            for kind in (0, 1):
                token_piece(i, kind).wait_recv()
                half_forward(2 * TOK + i * CH, CH, i * CH, kind)
            return 0

        lax.fori_loop(0, NCH, piece, 0)
        pl.semaphore_signal(done, inc=1, device_id=(other, d), device_id_type=MESH)
        activate(act, 2 * TOK, TOK)

        def term(r, put):
            grads(act, slice(0, 3 * TOK), pl.ds(0, 3 * TOK), lambda p: share_rs(d, p, r), put)

        reduce_scatter(term, rcv, rs_s, rs_r)
        for p in range(3):
            out[p] = acc[p, 0]
        low_cot.wait_send()
        low_nrm.wait_send()
        for i in range(NCH):
            for kind in (0, 1):
                token_piece(i, kind).wait_send()

    @pl.when(core == 1)
    def _():
        for p in range(3):
            weight_slice(p).start()
        mid_cot.start()
        load_rest()
        ld_tok.wait()
        normalise(TOK, TOK)
        mid_nrm.start()
        ld_cot.wait()
        ld_wg.wait()
        ld_wd.wait()
        forward(TOK, TOK, 0)
        activate(act, TOK, TOK)

        def term(r, put):
            grads(act, slice(TOK, 2 * TOK), mid, lambda p: share_rs(d, p, r), put)

        def gathering(k):
            for p in range(3):
                if k == 0:
                    weight_slice(p).wait_recv()
                    for step in range(3):
                        gather(p, 0, step).start()
                    if p == 1:
                        pl.semaphore_signal(
                            go, inc=1, device_id=(beside, df), device_id_type=MESH
                        )
                elif k == 1:
                    gather(p, 0, 0).wait_recv()
                    gather(p, 1, 1).start()
                    gather(p, 1, 2).start()
                elif k == 2:
                    gather(p, 0, 1).wait_recv()
                    gather(p, 2, 2).start()
                else:
                    gather(p, 1, 1).wait_recv()
                    gather(p, 3, 2).start()

        reduce_scatter(term, rcv, rs_s, rs_r, gathering)
        for p in range(3):
            out[p] = acc[p, 0]

        proj[...] = jnp.zeros_like(proj)
        both = pl.ds(0, 2 * TOK)
        low_cot.wait_recv()
        low_nrm.wait_recv()

        def partial(r, _):
            for p in range(2):
                j = share_ag(d, p, r)
                cols = pl.ds(pl.multiple_of(j * SL + p * 256, 256), 256)
                proj[:, 0:384] += jnp.dot(nrm[both, cols], wf[p, r], preferred_element_type=F32)
            proj[:, 384:576] += lax.dot_general(
                ctg[both, columns(share_ag(d, 2, r), SL)], wfd[r],
                (((1,), (1,)), ((), ())), preferred_element_type=F32,
            )
            return 0

        lax.fori_loop(0, 4, partial, 0)
        for src in range(4):
            for p in range(3):
                gather(p, src, 2).wait_recv()
            partial(src + 4, 0)
        activate(actf, 0, 2 * TOK)

        def foreign(r, put):
            grads(actf, slice(0, 2 * TOK), both, lambda p: flip(share_rs(d, p, r)), put)

        reduce_scatter(foreign, rcvf, rf_s, rf_r)
        for p in range(3):
            back[p] = acc[p, 0].astype(BF16)
        pl.semaphore_wait(done, 1)
        for p in range(3):
            returned(p).start()
        for p in range(3):
            returned(p).wait_recv()
            out[p] = out[p] + ret[p].astype(F32)

        mid_cot.wait_send()
        mid_nrm.wait_send()
        for p in range(3):
            weight_slice(p).wait_send()
            returned(p).wait_send()
            for src, step in gathers:
                gather(p, src, step).wait_send()


def local(tokens, cotangent, gain, gate_up, down):
    scale = 1.0 / math.sqrt(3 * TOK * 8)
    anywhere = pl.BlockSpec(memory_space=pl.ANY)
    vmem = pl.BlockSpec(memory_space=pltpu.VMEM)
    dma = pltpu.SemaphoreType.DMA
    sums = pl.pallas_call(
        kernel,
        out_shape=pltpu.VMEM((3, FB, SL), F32),
        in_specs=[anywhere, anywhere, vmem, anywhere, anywhere],
        out_specs=vmem,
        scratch_shapes=[
            pltpu.VMEM((3 * TOK, D), BF16),
            pltpu.VMEM((3 * TOK, D), BF16),
            pltpu.VMEM((D, 2 * FB), BF16),
            pltpu.VMEM((FB, D), BF16),
            pltpu.VMEM((2, 8, 256, 2 * FB), BF16),
            pltpu.VMEM((8, FB, SL), BF16),
            pltpu.VMEM((2 * TOK, 3 * FB), F32),
            pltpu.VMEM((3 * FB, 3 * TOK), BF16),
            pltpu.VMEM((3 * FB, 2 * TOK), BF16),
            pltpu.VMEM((3, 7, FB, SL), BF16),
            pltpu.VMEM((3, 7, FB, SL), BF16),
            pltpu.VMEM((3, 7, FB, SL), BF16),
            pltpu.VMEM((3, 4, FB, SL), F32),
            pltpu.VMEM((3, FB, SL), BF16),
            pltpu.VMEM((3, FB, SL), BF16),
            dma((4,)),
            dma((3,)), dma((3,)), dma((3, 7)), dma((3, 7)),
            dma((3, 7)), dma((3, 7)), dma((3, 7)), dma((3, 7)),
            dma((NCH, 2)), dma((NCH, 2)), dma((4,)), dma((4,)), dma((3,)), dma((3,)),
            pltpu.SemaphoreType.REGULAR, pltpu.SemaphoreType.REGULAR,
        ],
        compiler_params=pltpu.CompilerParams(
            collective_id=0, has_side_effects=True, vmem_limit_bytes=58 << 20
        ),
        name="grads",
    )(tokens, cotangent, gain.reshape(1, D), gate_up, down)
    return pl.pallas_call(
        functools.partial(finish, scale),
        out_shape=(
            jax.ShapeDtypeStruct((SL, 2 * FB), F32),
            jax.ShapeDtypeStruct((FB, SL), F32),
        ),
        in_specs=[vmem],
        out_specs=(vmem, vmem),
        name="scaled",
    )(pltpu.with_memory_space_constraint(sums, pltpu.VMEM))


def solution(mesh):
    in_specs = (P(("blk", "dp"), None), P(("blk", "dp"), None), P(), P(None, "blk"), P("blk", None))
    out_specs = (P("dp", "blk"), P("blk", "dp"))
    return jax.shard_map(local, mesh=mesh, in_specs=in_specs, out_specs=out_specs, check_vma=False)
```

```python
import functools
import math

import jax
import jax.numpy as jnp
from jax import lax
from jax.experimental import pallas as pl
from jax.experimental.pallas import tpu as pltpu
from jax.sharding import PartitionSpec as P

MESH = pl.DeviceIdType.MESH
F32 = jnp.float32
BF16 = jnp.bfloat16

TOK = 256
D = 4096
FB = 192
SL = D // 8
CH = 64
NCH = TOK // CH

HALF = (slice(0, FB // 2), slice(FB // 2, FB))
ORDERS = (("a", "b", "y"), ("b", "y", "a"), ("y", "a", "b"))


def flip(v):
    return v + 1 - 2 * lax.rem(v, 2)


def moved(d, toggle):
    x, y = d // 2, lax.rem(d, 2)
    x = x + toggle["a"] * (1 - 2 * lax.rem(x, 2))
    x = lax.rem(x + toggle["b"] * (2 * lax.rem(x, 2) - 1) + 4, 4)
    y = y + toggle["y"] * (1 - 2 * y)
    return 2 * x + y


def partner(d, dim):
    return moved(d, {name: int(name == dim) for name in "aby"})


def share_rs(d, p, r):
    o = ORDERS[p]
    return moved(d, {o[0]: r // 4, o[1]: lax.rem(r // 2, 2), o[2]: lax.rem(r, 2)})


def share_ag(d, p, r):
    o = ORDERS[p]
    return moved(d, {o[2]: r // 4, o[1]: lax.rem(r // 2, 2), o[0]: lax.rem(r, 2)})


def columns(j, width):
    return pl.ds(pl.multiple_of(j * width, width), width)


def finish(scale, sums, o_gu, o_dn):
    o_gu[:, 0:FB] = (sums[0] * scale).T
    o_gu[:, FB:2 * FB] = (sums[1] * scale).T
    o_dn[...] = sums[2] * scale


def kernel(
    tok, cot, gain, gu, dn,
    out,
    nrm, ctg, wg, wd, wf, wfd, proj, act, actf, snd, rcv, rcvf, acc, back, ret,
    ld_sem, ws_s, ws_r, ag_s, ag_r, rs_s, rs_r, rf_s, rf_r,
    tk_s, tk_r, in_s, in_r, rt_s, rt_r, go, done,
):
    b = lax.axis_index("blk")
    d = lax.axis_index("dp")
    core = lax.rem(b, 2)
    n_blk = 32
    nxt = lax.rem(b + 2, n_blk)
    prv = lax.rem(b + n_blk - 2, n_blk)
    other = flip(b)
    beside = lax.rem(b + n_blk - 1 + 2 * core, n_blk)
    df = flip(d)
    own = pl.ds(pl.multiple_of(core * TOK, TOK), TOK)

    def load(i, src, dst):
        return pltpu.make_async_copy(src, dst, ld_sem.at[i])

    def remote(src, dst, ss, rs, tb, td):
        return pltpu.make_async_remote_copy(
            src_ref=src, dst_ref=dst, send_sem=ss, recv_sem=rs,
            device_id=(tb, td), device_id_type=MESH,
        )

    ld_tok = load(0, tok, nrm.at[own])
    ld_cot = load(1, cot, ctg.at[own])
    ld_wg = load(2, gu, wg)
    ld_wd = load(3, dn, wd)
    ld_tok.start()

    def load_rest():
        ld_cot.start()
        ld_wg.start()
        ld_wd.start()

    barrier = pltpu.get_barrier_semaphore()
    greeted = [(other, d), (nxt, df), (prv, df), (beside, df)] + [(b, partner(d, k)) for k in "aby"]
    for tb, td in greeted:
        pl.semaphore_signal(barrier, inc=1, device_id=(tb, td), device_id_type=MESH)
    pl.semaphore_wait(barrier, len(greeted))

    def weight_slice(p):
        if p == 2:
            return remote(dn.at[:, columns(df, SL)], wfd.at[0], ws_s.at[2], ws_r.at[2], nxt, df)
        rows = pl.ds(pl.multiple_of(df * SL + p * 256, 256), 256)
        return remote(gu.at[rows, :], wf.at[p, 0], ws_s.at[p], ws_r.at[p], nxt, df)

    def gather(p, src, step):
        ref = wfd if p == 2 else wf.at[p]
        dst = src + 2 ** step
        return remote(
            ref.at[src], ref.at[dst], ag_s.at[p, dst - 1], ag_r.at[p, dst - 1],
            b, partner(d, ORDERS[p][step]),
        )

    gathers = [(0, 0), (0, 1), (0, 2), (1, 1), (1, 2), (2, 2), (3, 2)]

    def token_piece(i, kind):
        here = pl.ds(pl.multiple_of(i * CH, CH), CH)
        there = pl.ds(pl.multiple_of(2 * TOK + i * CH, CH), CH)
        if kind == 0:
            return remote(cot.at[here], ctg.at[there], tk_s.at[i, 0], tk_r.at[i, 0], prv, df)
        return remote(nrm.at[here], nrm.at[there], tk_s.at[i, 1], tk_r.at[i, 1], prv, df)

    low, mid = pl.ds(0, TOK), pl.ds(TOK, TOK)
    low_cot = remote(cot, ctg.at[low], in_s.at[0], in_r.at[0], other, d)
    low_nrm = remote(nrm.at[low], nrm.at[low], in_s.at[1], in_r.at[1], other, d)
    mid_cot = remote(cot, ctg.at[mid], in_s.at[2], in_r.at[2], other, d)
    mid_nrm = remote(nrm.at[mid], nrm.at[mid], in_s.at[3], in_r.at[3], other, d)

    def returned(p):
        return remote(back.at[p], ret.at[p], rt_s.at[p], rt_r.at[p], prv, df)

    def normalise(row0, n):
        def body(i, _):
            rows = pl.ds(pl.multiple_of(row0 + i * 16, 16), 16)
            v = nrm[rows, :].astype(F32)
            inv = lax.rsqrt(jnp.mean(v * v, axis=-1, keepdims=True) + 1e-06)
            nrm[rows, :] = (v * inv * gain[...]).astype(BF16)
            return 0

        lax.fori_loop(0, n // 16, body, 0)

    def half_forward(row0, n, to, kind):
        rows = pl.ds(pl.multiple_of(row0, CH), n)
        dst = pl.ds(pl.multiple_of(to, CH), n)
        if kind:
            proj[dst, 0:384] = jnp.dot(nrm[rows, :], wg[...], preferred_element_type=F32)
        else:
            proj[dst, 384:576] = lax.dot_general(
                ctg[rows, :], wd[...], (((1,), (1,)), ((), ())), preferred_element_type=F32
            )

    def forward(row0, n, to):
        half_forward(row0, n, to, 0)
        half_forward(row0, n, to, 1)

    def activate(dst, col, n):
        cols = slice(col, col + n)
        t = proj[0:n].T
        gate, up, bk = t[0:FB], t[FB:2 * FB], t[2 * FB:3 * FB]
        s = jax.nn.sigmoid(gate)
        dst[0:FB, cols] = (bk * up * (s * (1.0 + gate * (1.0 - s)))).astype(BF16)
        dst[FB:2 * FB, cols] = (bk * gate * s).astype(BF16)
        dst[2 * FB:3 * FB, cols] = (gate * s * up).astype(BF16)

    def reduce_scatter(term, r_ref, s_sem, r_sem, beside_it=lambda k: None):
        def copy(p, slot, step):
            return remote(
                snd.at[p, slot], r_ref.at[p, slot], s_sem.at[p, slot], r_sem.at[p, slot],
                b, partner(d, ORDERS[p][step]),
            )

        def half(p, slot, step, h):
            k = 4 + 2 * (slot - 4) + h
            return remote(
                snd.at[p, slot, HALF[h]], r_ref.at[p, slot, HALF[h]],
                s_sem.at[p, k], r_sem.at[p, k], b, partner(d, ORDERS[p][step]),
            )

        def first(i, _):
            q = 3 - 2 * lax.rem(i, 2) - i // 2

            def put(p, v):
                snd[p, q] = v.astype(BF16)
                copy(p, q, 0).start()

            term(q + 4, put)
            return 0

        def kept(i, _):
            q = 3 - 2 * lax.rem(i, 2) - i // 2

            def put(p, v):
                acc[p, q] = v

            term(q, put)
            return 0

        lax.fori_loop(0, 4, first, 0)
        lax.fori_loop(0, 4, kept, 0)
        for q in (3, 1, 2, 0):
            for p in range(3):
                copy(p, q, 0).wait_recv()
                for h in range(2):
                    rows = HALF[h]
                    v = acc[p, q, rows] + r_ref[p, q, rows].astype(F32)
                    if q >= 2:
                        snd[p, q + 2, rows] = v.astype(BF16)
                        half(p, q + 2, 1, h).start()
                    else:
                        acc[p, q, rows] = v
        beside_it(1)
        for h in range(2):
            rows = HALF[h]
            for p in range(3):
                half(p, 5, 1, h).wait_recv()
                snd[p, 6, rows] = (acc[p, 1, rows] + r_ref[p, 5, rows].astype(F32)).astype(BF16)
                half(p, 6, 2, h).start()
        beside_it(2)
        for slot, step in ((4, 1), (6, 2)):
            for h in range(2):
                rows = HALF[h]
                for p in range(3):
                    half(p, slot, step, h).wait_recv()
                    acc[p, 0, rows] = acc[p, 0, rows] + r_ref[p, slot, rows].astype(F32)
        beside_it(3)
        for p in range(3):
            for slot in range(4):
                copy(p, slot, 0).wait_send()
            for slot, step in ((4, 1), (5, 1), (6, 2)):
                for h in range(2):
                    half(p, slot, step, h).wait_send()

    def grads(a_ref, a_cols, tok_rows, share, put):
        for p in range(3):
            x = ctg if p == 2 else nrm
            put(p, jnp.dot(
                a_ref[p * FB:(p + 1) * FB, a_cols],
                x[tok_rows, columns(share(p), SL)],
                preferred_element_type=F32,
            ))

    @pl.when(core == 0)
    def _():
        low_cot.start()
        load_rest()
        ld_tok.wait()
        normalise(0, TOK)
        low_nrm.start()
        pl.semaphore_wait(go, 1)
        for i in range(NCH):
            token_piece(i, 0).start()
            token_piece(i, 1).start()
        ld_cot.wait()
        ld_wg.wait()
        ld_wd.wait()
        forward(0, TOK, 0)
        activate(act, 0, TOK)
        mid_cot.wait_recv()
        mid_nrm.wait_recv()
        forward(TOK, TOK, 0)
        activate(act, TOK, TOK)

        def piece(i, _):
            for kind in (0, 1):
                token_piece(i, kind).wait_recv()
                half_forward(2 * TOK + i * CH, CH, i * CH, kind)
            return 0

        lax.fori_loop(0, NCH, piece, 0)
        pl.semaphore_signal(done, inc=1, device_id=(other, d), device_id_type=MESH)
        activate(act, 2 * TOK, TOK)

        def term(r, put):
            grads(act, slice(0, 3 * TOK), pl.ds(0, 3 * TOK), lambda p: share_rs(d, p, r), put)

        reduce_scatter(term, rcv, rs_s, rs_r)
        for p in range(3):
            out[p] = acc[p, 0]
        low_cot.wait_send()
        low_nrm.wait_send()
        for i in range(NCH):
            for kind in (0, 1):
                token_piece(i, kind).wait_send()

    @pl.when(core == 1)
    def _():
        for p in range(3):
            weight_slice(p).start()
        mid_cot.start()
        load_rest()
        ld_tok.wait()
        normalise(TOK, TOK)
        mid_nrm.start()
        ld_cot.wait()
        ld_wg.wait()
        ld_wd.wait()
        forward(TOK, TOK, 0)
        activate(act, TOK, TOK)

        def term(r, put):
            grads(act, slice(TOK, 2 * TOK), mid, lambda p: share_rs(d, p, r), put)

        def gathering(k):
            for p in range(3):
                if k == 0:
                    weight_slice(p).wait_recv()
                    for step in range(3):
                        gather(p, 0, step).start()
                    if p == 1:
                        pl.semaphore_signal(
                            go, inc=1, device_id=(beside, df), device_id_type=MESH
                        )
                elif k == 1:
                    gather(p, 0, 0).wait_recv()
                    gather(p, 1, 1).start()
                    gather(p, 1, 2).start()
                elif k == 2:
                    gather(p, 0, 1).wait_recv()
                    gather(p, 2, 2).start()
                else:
                    gather(p, 1, 1).wait_recv()
                    gather(p, 3, 2).start()

        gathering(0)
        reduce_scatter(term, rcv, rs_s, rs_r, gathering)
        for p in range(3):
            out[p] = acc[p, 0]

        proj[...] = jnp.zeros_like(proj)
        both = pl.ds(0, 2 * TOK)
        low_cot.wait_recv()
        low_nrm.wait_recv()

        def partial(r, _):
            for p in range(2):
                j = share_ag(d, p, r)
                cols = pl.ds(pl.multiple_of(j * SL + p * 256, 256), 256)
                proj[:, 0:384] += jnp.dot(nrm[both, cols], wf[p, r], preferred_element_type=F32)
            proj[:, 384:576] += lax.dot_general(
                ctg[both, columns(share_ag(d, 2, r), SL)], wfd[r],
                (((1,), (1,)), ((), ())), preferred_element_type=F32,
            )
            return 0

        lax.fori_loop(0, 4, partial, 0)
        for src in range(4):
            for p in range(3):
                gather(p, src, 2).wait_recv()
            partial(src + 4, 0)
        activate(actf, 0, 2 * TOK)

        def foreign(r, put):
            grads(actf, slice(0, 2 * TOK), both, lambda p: flip(share_rs(d, p, r)), put)

        reduce_scatter(foreign, rcvf, rf_s, rf_r)
        for p in range(3):
            back[p] = acc[p, 0].astype(BF16)
        pl.semaphore_wait(done, 1)
        for p in range(3):
            returned(p).start()
        for p in range(3):
            returned(p).wait_recv()
            out[p] = out[p] + ret[p].astype(F32)

        mid_cot.wait_send()
        mid_nrm.wait_send()
        for p in range(3):
            weight_slice(p).wait_send()
            returned(p).wait_send()
            for src, step in gathers:
                gather(p, src, step).wait_send()


def local(tokens, cotangent, gain, gate_up, down):
    scale = 1.0 / math.sqrt(3 * TOK * 8)
    anywhere = pl.BlockSpec(memory_space=pl.ANY)
    vmem = pl.BlockSpec(memory_space=pltpu.VMEM)
    dma = pltpu.SemaphoreType.DMA
    sums = pl.pallas_call(
        kernel,
        out_shape=pltpu.VMEM((3, FB, SL), F32),
        in_specs=[anywhere, anywhere, vmem, anywhere, anywhere],
        out_specs=vmem,
        scratch_shapes=[
            pltpu.VMEM((3 * TOK, D), BF16),
            pltpu.VMEM((3 * TOK, D), BF16),
            pltpu.VMEM((D, 2 * FB), BF16),
            pltpu.VMEM((FB, D), BF16),
            pltpu.VMEM((2, 8, 256, 2 * FB), BF16),
            pltpu.VMEM((8, FB, SL), BF16),
            pltpu.VMEM((2 * TOK, 3 * FB), F32),
            pltpu.VMEM((3 * FB, 3 * TOK), BF16),
            pltpu.VMEM((3 * FB, 2 * TOK), BF16),
            pltpu.VMEM((3, 7, FB, SL), BF16),
            pltpu.VMEM((3, 7, FB, SL), BF16),
            pltpu.VMEM((3, 7, FB, SL), BF16),
            pltpu.VMEM((3, 4, FB, SL), F32),
            pltpu.VMEM((3, FB, SL), BF16),
            pltpu.VMEM((3, FB, SL), BF16),
            dma((4,)),
            dma((3,)), dma((3,)), dma((3, 7)), dma((3, 7)),
            dma((3, 10)), dma((3, 10)), dma((3, 10)), dma((3, 10)),
            dma((NCH, 2)), dma((NCH, 2)), dma((4,)), dma((4,)), dma((3,)), dma((3,)),
            pltpu.SemaphoreType.REGULAR, pltpu.SemaphoreType.REGULAR,
        ],
        compiler_params=pltpu.CompilerParams(
            collective_id=0, has_side_effects=True, vmem_limit_bytes=58 << 20
        ),
        name="grads",
    )(tokens, cotangent, gain.reshape(1, D), gate_up, down)
    return pl.pallas_call(
        functools.partial(finish, scale),
        out_shape=(
            jax.ShapeDtypeStruct((SL, 2 * FB), F32),
            jax.ShapeDtypeStruct((FB, SL), F32),
        ),
        in_specs=[vmem],
        out_specs=(vmem, vmem),
        name="scaled",
    )(pltpu.with_memory_space_constraint(sums, pltpu.VMEM))


def solution(mesh):
    in_specs = (P(("blk", "dp"), None), P(("blk", "dp"), None), P(), P(None, "blk"), P("blk", None))
    out_specs = (P("dp", "blk"), P("blk", "dp"))
    return jax.shard_map(local, mesh=mesh, in_specs=in_specs, out_specs=out_specs, check_vma=False)
```

```python
import functools
import math

import jax
import jax.numpy as jnp
from jax import lax
from jax.experimental import pallas as pl
from jax.experimental.pallas import tpu as pltpu
from jax.sharding import PartitionSpec as P

MESH = pl.DeviceIdType.MESH
F32 = jnp.float32
BF16 = jnp.bfloat16

TOK = 256
D = 4096
FB = 192
SL = D // 8
CH = 64
NCH = TOK // CH

HALF = (slice(0, FB // 2), slice(FB // 2, FB))
ORDERS = (("a", "b", "y"), ("b", "y", "a"), ("y", "a", "b"))


def flip(v):
    return v + 1 - 2 * lax.rem(v, 2)


def moved(d, toggle):
    x, y = d // 2, lax.rem(d, 2)
    x = x + toggle["a"] * (1 - 2 * lax.rem(x, 2))
    x = lax.rem(x + toggle["b"] * (2 * lax.rem(x, 2) - 1) + 4, 4)
    y = y + toggle["y"] * (1 - 2 * y)
    return 2 * x + y


def partner(d, dim):
    return moved(d, {name: int(name == dim) for name in "aby"})


def share_rs(d, p, r):
    o = ORDERS[p]
    return moved(d, {o[0]: r // 4, o[1]: lax.rem(r // 2, 2), o[2]: lax.rem(r, 2)})


def share_ag(d, p, r):
    o = ORDERS[p]
    return moved(d, {o[2]: r // 4, o[1]: lax.rem(r // 2, 2), o[0]: lax.rem(r, 2)})


def columns(j, width):
    return pl.ds(pl.multiple_of(j * width, width), width)


def finish(scale, sums, o_gu, o_dn):
    o_gu[:, 0:FB] = (sums[0] * scale).T
    o_gu[:, FB:2 * FB] = (sums[1] * scale).T
    o_dn[...] = sums[2] * scale


def kernel(
    tok, cot, gain, gu, dn,
    out,
    nrm, ctg, wg, wd, wf, wfd, proj, act, actf, snd, rcv, rcvf, acc, early, back, ret,
    ld_sem, ws_s, ws_r, ag_s, ag_r, rs_s, rs_r, rf_s, rf_r,
    tk_s, tk_r, in_s, in_r, rt_s, rt_r, go, done,
):
    b = lax.axis_index("blk")
    d = lax.axis_index("dp")
    core = lax.rem(b, 2)
    n_blk = 32
    nxt = lax.rem(b + 2, n_blk)
    prv = lax.rem(b + n_blk - 2, n_blk)
    other = flip(b)
    beside = lax.rem(b + n_blk - 1 + 2 * core, n_blk)
    df = flip(d)
    own = pl.ds(pl.multiple_of(core * TOK, TOK), TOK)

    def load(i, src, dst):
        return pltpu.make_async_copy(src, dst, ld_sem.at[i])

    def remote(src, dst, ss, rs, tb, td):
        return pltpu.make_async_remote_copy(
            src_ref=src, dst_ref=dst, send_sem=ss, recv_sem=rs,
            device_id=(tb, td), device_id_type=MESH,
        )

    ld_tok = load(0, tok, nrm.at[own])
    ld_cot = load(1, cot, ctg.at[own])
    ld_wg = load(2, gu, wg)
    ld_wd = load(3, dn, wd)
    ld_tok.start()

    def load_rest():
        ld_cot.start()
        ld_wg.start()
        ld_wd.start()

    barrier = pltpu.get_barrier_semaphore()
    greeted = [(other, d), (nxt, df), (prv, df), (beside, df)] + [(b, partner(d, k)) for k in "aby"]
    for tb, td in greeted:
        pl.semaphore_signal(barrier, inc=1, device_id=(tb, td), device_id_type=MESH)
    pl.semaphore_wait(barrier, len(greeted))

    def weight_slice(p):
        if p == 2:
            return remote(dn.at[:, columns(df, SL)], wfd.at[0], ws_s.at[2], ws_r.at[2], nxt, df)
        rows = pl.ds(pl.multiple_of(df * SL + p * 256, 256), 256)
        return remote(gu.at[rows, :], wf.at[p, 0], ws_s.at[p], ws_r.at[p], nxt, df)

    def gather(p, src, step):
        ref = wfd if p == 2 else wf.at[p]
        dst = src + 2 ** step
        return remote(
            ref.at[src], ref.at[dst], ag_s.at[p, dst - 1], ag_r.at[p, dst - 1],
            b, partner(d, ORDERS[p][step]),
        )

    gathers = [(0, 0), (0, 1), (0, 2), (1, 1), (1, 2), (2, 2), (3, 2)]

    def token_piece(i, kind):
        here = pl.ds(pl.multiple_of(i * CH, CH), CH)
        there = pl.ds(pl.multiple_of(2 * TOK + i * CH, CH), CH)
        if kind == 0:
            return remote(cot.at[here], ctg.at[there], tk_s.at[i, 0], tk_r.at[i, 0], prv, df)
        return remote(nrm.at[here], nrm.at[there], tk_s.at[i, 1], tk_r.at[i, 1], prv, df)

    low, mid = pl.ds(0, TOK), pl.ds(TOK, TOK)
    low_cot = remote(cot, ctg.at[low], in_s.at[0], in_r.at[0], other, d)
    low_nrm = remote(nrm.at[low], nrm.at[low], in_s.at[1], in_r.at[1], other, d)
    mid_cot = remote(cot, ctg.at[mid], in_s.at[2], in_r.at[2], other, d)
    mid_nrm = remote(nrm.at[mid], nrm.at[mid], in_s.at[3], in_r.at[3], other, d)

    def returned(p):
        return remote(back.at[p], ret.at[p], rt_s.at[p], rt_r.at[p], prv, df)

    def normalise(row0, n):
        def body(i, _):
            rows = pl.ds(pl.multiple_of(row0 + i * 16, 16), 16)
            v = nrm[rows, :].astype(F32)
            inv = lax.rsqrt(jnp.mean(v * v, axis=-1, keepdims=True) + 1e-06)
            nrm[rows, :] = (v * inv * gain[...]).astype(BF16)
            return 0

        lax.fori_loop(0, n // 16, body, 0)

    def half_forward(row0, n, to, kind):
        rows = pl.ds(pl.multiple_of(row0, CH), n)
        dst = pl.ds(pl.multiple_of(to, CH), n)
        if kind:
            proj[dst, 0:384] = jnp.dot(nrm[rows, :], wg[...], preferred_element_type=F32)
        else:
            proj[dst, 384:576] = lax.dot_general(
                ctg[rows, :], wd[...], (((1,), (1,)), ((), ())), preferred_element_type=F32
            )

    def forward(row0, n, to):
        half_forward(row0, n, to, 0)
        half_forward(row0, n, to, 1)

    def activate(dst, col, n):
        cols = slice(col, col + n)
        t = proj[0:n].T
        gate, up, bk = t[0:FB], t[FB:2 * FB], t[2 * FB:3 * FB]
        s = jax.nn.sigmoid(gate)
        dst[0:FB, cols] = (bk * up * (s * (1.0 + gate * (1.0 - s)))).astype(BF16)
        dst[FB:2 * FB, cols] = (bk * gate * s).astype(BF16)
        dst[2 * FB:3 * FB, cols] = (gate * s * up).astype(BF16)

    def reduce_scatter(term, r_ref, s_sem, r_sem, beside_it=lambda k: None):
        def copy(p, slot, step):
            return remote(
                snd.at[p, slot], r_ref.at[p, slot], s_sem.at[p, slot], r_sem.at[p, slot],
                b, partner(d, ORDERS[p][step]),
            )

        def half(p, slot, step, h):
            k = 4 + 2 * (slot - 4) + h
            return remote(
                snd.at[p, slot, HALF[h]], r_ref.at[p, slot, HALF[h]],
                s_sem.at[p, k], r_sem.at[p, k], b, partner(d, ORDERS[p][step]),
            )

        def first(i, _):
            q = 3 - 2 * lax.rem(i, 2) - i // 2

            def put(p, v):
                snd[p, q] = v.astype(BF16)
                copy(p, q, 0).start()

            term(q + 4, put)
            return 0

        def kept(i, _):
            q = 3 - 2 * lax.rem(i, 2) - i // 2

            def put(p, v):
                acc[p, q] = v

            term(q, put)
            return 0

        lax.fori_loop(0, 4, first, 0)
        lax.fori_loop(0, 4, kept, 0)
        for q in (3, 1, 2, 0):
            for p in range(3):
                copy(p, q, 0).wait_recv()
                for h in range(2):
                    rows = HALF[h]
                    v = acc[p, q, rows] + r_ref[p, q, rows].astype(F32)
                    if q >= 2:
                        snd[p, q + 2, rows] = v.astype(BF16)
                        half(p, q + 2, 1, h).start()
                    else:
                        acc[p, q, rows] = v
        beside_it(1)
        for h in range(2):
            rows = HALF[h]
            for p in range(3):
                half(p, 5, 1, h).wait_recv()
                snd[p, 6, rows] = (acc[p, 1, rows] + r_ref[p, 5, rows].astype(F32)).astype(BF16)
                half(p, 6, 2, h).start()
        beside_it(2)
        for slot, step in ((4, 1), (6, 2)):
            for h in range(2):
                rows = HALF[h]
                for p in range(3):
                    half(p, slot, step, h).wait_recv()
                    acc[p, 0, rows] = acc[p, 0, rows] + r_ref[p, slot, rows].astype(F32)
        beside_it(3)
        for p in range(3):
            for slot in range(4):
                copy(p, slot, 0).wait_send()
            for slot, step in ((4, 1), (5, 1), (6, 2)):
                for h in range(2):
                    half(p, slot, step, h).wait_send()

    def grads(a_ref, a_cols, tok_rows, share, put):
        for p in range(3):
            x = ctg if p == 2 else nrm
            put(p, jnp.dot(
                a_ref[p * FB:(p + 1) * FB, a_cols],
                x[tok_rows, columns(share(p), SL)],
                preferred_element_type=F32,
            ))

    @pl.when(core == 0)
    def _():
        low_cot.start()
        load_rest()
        ld_tok.wait()
        normalise(0, TOK)
        low_nrm.start()
        pl.semaphore_wait(go, 1)
        for i in range(NCH):
            token_piece(i, 0).start()
            token_piece(i, 1).start()
        ld_cot.wait()
        ld_wg.wait()
        ld_wd.wait()
        forward(0, TOK, 0)
        activate(act, 0, TOK)
        mid_cot.wait_recv()
        mid_nrm.wait_recv()
        forward(TOK, TOK, 0)
        activate(act, TOK, TOK)

        def here(r, _):
            def put(p, v):
                early[p, r] = v

            grads(act, slice(0, 2 * TOK), pl.ds(0, 2 * TOK), lambda p: share_rs(d, p, r), put)
            return 0

        lax.fori_loop(0, 8, here, 0)

        def piece(i, _):
            for kind in (0, 1):
                token_piece(i, kind).wait_recv()
                half_forward(2 * TOK + i * CH, CH, i * CH, kind)
            return 0

        lax.fori_loop(0, NCH, piece, 0)
        pl.semaphore_signal(done, inc=1, device_id=(other, d), device_id_type=MESH)
        activate(act, 2 * TOK, TOK)

        def term(r, put):
            def add(p, v):
                put(p, early[p, r] + v)

            last = pl.ds(2 * TOK, TOK)
            grads(act, slice(2 * TOK, 3 * TOK), last, lambda p: share_rs(d, p, r), add)

        reduce_scatter(term, rcv, rs_s, rs_r)
        for p in range(3):
            out[p] = acc[p, 0]
        low_cot.wait_send()
        low_nrm.wait_send()
        for i in range(NCH):
            for kind in (0, 1):
                token_piece(i, kind).wait_send()

    @pl.when(core == 1)
    def _():
        for p in range(3):
            weight_slice(p).start()
        mid_cot.start()
        load_rest()
        ld_tok.wait()
        normalise(TOK, TOK)
        mid_nrm.start()
        ld_cot.wait()
        ld_wg.wait()
        ld_wd.wait()
        forward(TOK, TOK, 0)
        activate(act, TOK, TOK)

        def term(r, put):
            grads(act, slice(TOK, 2 * TOK), mid, lambda p: share_rs(d, p, r), put)

        def gathering(k):
            for p in range(3):
                if k == 0:
                    weight_slice(p).wait_recv()
                    for step in range(3):
                        gather(p, 0, step).start()
                    if p == 1:
                        pl.semaphore_signal(
                            go, inc=1, device_id=(beside, df), device_id_type=MESH
                        )
                elif k == 1:
                    gather(p, 0, 0).wait_recv()
                    gather(p, 1, 1).start()
                    gather(p, 1, 2).start()
                elif k == 2:
                    gather(p, 0, 1).wait_recv()
                    gather(p, 2, 2).start()
                else:
                    gather(p, 1, 1).wait_recv()
                    gather(p, 3, 2).start()

        gathering(0)
        reduce_scatter(term, rcv, rs_s, rs_r, gathering)
        for p in range(3):
            out[p] = acc[p, 0]

        proj[...] = jnp.zeros_like(proj)
        both = pl.ds(0, 2 * TOK)
        low_cot.wait_recv()
        low_nrm.wait_recv()

        def partial(r, _):
            for p in range(2):
                j = share_ag(d, p, r)
                cols = pl.ds(pl.multiple_of(j * SL + p * 256, 256), 256)
                proj[:, 0:384] += jnp.dot(nrm[both, cols], wf[p, r], preferred_element_type=F32)
            proj[:, 384:576] += lax.dot_general(
                ctg[both, columns(share_ag(d, 2, r), SL)], wfd[r],
                (((1,), (1,)), ((), ())), preferred_element_type=F32,
            )
            return 0

        lax.fori_loop(0, 4, partial, 0)
        for src in range(4):
            for p in range(3):
                gather(p, src, 2).wait_recv()
            partial(src + 4, 0)
        activate(actf, 0, 2 * TOK)

        def foreign(r, put):
            grads(actf, slice(0, 2 * TOK), both, lambda p: flip(share_rs(d, p, r)), put)

        reduce_scatter(foreign, rcvf, rf_s, rf_r)
        for p in range(3):
            back[p] = acc[p, 0].astype(BF16)
        pl.semaphore_wait(done, 1)
        for p in range(3):
            returned(p).start()
        for p in range(3):
            returned(p).wait_recv()
            out[p] = out[p] + ret[p].astype(F32)

        mid_cot.wait_send()
        mid_nrm.wait_send()
        for p in range(3):
            weight_slice(p).wait_send()
            returned(p).wait_send()
            for src, step in gathers:
                gather(p, src, step).wait_send()


def local(tokens, cotangent, gain, gate_up, down):
    scale = 1.0 / math.sqrt(3 * TOK * 8)
    anywhere = pl.BlockSpec(memory_space=pl.ANY)
    vmem = pl.BlockSpec(memory_space=pltpu.VMEM)
    dma = pltpu.SemaphoreType.DMA
    sums = pl.pallas_call(
        kernel,
        out_shape=pltpu.VMEM((3, FB, SL), F32),
        in_specs=[anywhere, anywhere, vmem, anywhere, anywhere],
        out_specs=vmem,
        scratch_shapes=[
            pltpu.VMEM((3 * TOK, D), BF16),
            pltpu.VMEM((3 * TOK, D), BF16),
            pltpu.VMEM((D, 2 * FB), BF16),
            pltpu.VMEM((FB, D), BF16),
            pltpu.VMEM((2, 8, 256, 2 * FB), BF16),
            pltpu.VMEM((8, FB, SL), BF16),
            pltpu.VMEM((2 * TOK, 3 * FB), F32),
            pltpu.VMEM((3 * FB, 3 * TOK), BF16),
            pltpu.VMEM((3 * FB, 2 * TOK), BF16),
            pltpu.VMEM((3, 7, FB, SL), BF16),
            pltpu.VMEM((3, 7, FB, SL), BF16),
            pltpu.VMEM((3, 7, FB, SL), BF16),
            pltpu.VMEM((3, 4, FB, SL), F32),
            pltpu.VMEM((3, 8, FB, SL), F32),
            pltpu.VMEM((3, FB, SL), BF16),
            pltpu.VMEM((3, FB, SL), BF16),
            dma((4,)),
            dma((3,)), dma((3,)), dma((3, 7)), dma((3, 7)),
            dma((3, 10)), dma((3, 10)), dma((3, 10)), dma((3, 10)),
            dma((NCH, 2)), dma((NCH, 2)), dma((4,)), dma((4,)), dma((3,)), dma((3,)),
            pltpu.SemaphoreType.REGULAR, pltpu.SemaphoreType.REGULAR,
        ],
        compiler_params=pltpu.CompilerParams(
            collective_id=0, has_side_effects=True, vmem_limit_bytes=58 << 20
        ),
        name="grads",
    )(tokens, cotangent, gain.reshape(1, D), gate_up, down)
    return pl.pallas_call(
        functools.partial(finish, scale),
        out_shape=(
            jax.ShapeDtypeStruct((SL, 2 * FB), F32),
            jax.ShapeDtypeStruct((FB, SL), F32),
        ),
        in_specs=[vmem],
        out_specs=(vmem, vmem),
        name="scaled",
    )(pltpu.with_memory_space_constraint(sums, pltpu.VMEM))


def solution(mesh):
    in_specs = (P(("blk", "dp"), None), P(("blk", "dp"), None), P(), P(None, "blk"), P("blk", None))
    out_specs = (P("dp", "blk"), P("blk", "dp"))
    return jax.shard_map(local, mesh=mesh, in_specs=in_specs, out_specs=out_specs, check_vma=False)
```
